32 devices in a mesh: rep: 8 (over y, x, core), et: 4 (over z).
Axes of the slice: x: 2, y: 2, z: 4, core: 2. Of those that a mesh axis runs over, the one named last changes fastest.
Arguments:
- tokens: bfloat16 [4096, 2048], P(('rep', 'et')), parts along dimension 0, may hold values from -6 to 6
- expert_ids: int32 [4096, 2], P(('rep', 'et')), parts along dimension 0, may hold values from 0 to 7, as said below
- route_logits: float32 [4096, 2], P(('rep', 'et')), parts along dimension 0, may hold values from -3 to 3
- w_gate: bfloat16 [2, 7168, 2048], P(None, 'et'), may hold values from -0.125 to 0.125
- w_up: bfloat16 [2, 7168, 2048], P(None, 'et'), may hold values from -0.125 to 0.125
- w_down: bfloat16 [2, 7168, 2048], P(None, 'et'), may hold values from -0.0625 to 0.0625
Outputs:
- mixed: bfloat16 [4096, 2048], P(('rep', 'et')), parts along dimension 0
The draws below stay inside these ranges and needn't reach their ends.
There are 8 independent parts, one for each index of `rep`. The reference program is written for one: setup_inputs(seed, part) draws one part's arguments, and reference() takes and returns one part's arrays. A program takes and returns all parts, laid end to end along the dimension named above; an argument that names none is the same for every part. Nothing has to cross between parts.
Inputs may be any that keep to these rules, and one draw needn't show every extreme that they name: `expert_ids`: each row names two different experts. Within each aligned block of 128 rows (the rows of one device), no expert is named by more than 48 rows, and experts 0 and 1 are each named by exactly 48 rows.
All inputs are finite; a program needn't handle non-finite values.
Results may differ from the reference program's by a relative error of at most 0.015.
Values may be sent and summed in bfloat16 or wider, within the bound.
A program may use at most 128 MiB of HBM per device.

```python
import jax
import jax.numpy as jnp
from jax import lax

D = 2048
FF = 7168
EXPERTS = 8
EXP_WIN = 2
TOK_DEV = 128
CAP = 48
TOKENS = 512
N_ET = 4


def route_block(key):
    key_order, key_rank, key_rows, key_flip = jax.random.split(key, 4)
    order = jax.random.permutation(key_order, EXPERTS).astype(jnp.int32)
    others = EXPERTS - 2
    remaining = 2 * TOK_DEV - 2 * CAP
    base_count = remaining // others
    extra_count = remaining % others
    other_rank = jax.random.permutation(key_rank, others).astype(jnp.int32)
    numbers = jnp.arange(EXPERTS, dtype=jnp.int32)
    rank_of = other_rank[jnp.clip(numbers - 2, 0, others - 1)]
    counts_by_id = jnp.where(numbers < 2, jnp.int32(CAP), base_count + (rank_of < extra_count).astype(jnp.int32))
    counts_in_order = counts_by_id[order]
    ends = jnp.cumsum(counts_in_order).astype(jnp.int32)
    positions = jnp.arange(2 * TOK_DEV, dtype=jnp.int32)
    group_index = jnp.sum((positions[:, None] >= ends[None, :]).astype(jnp.int32), axis=1)
    labels = order[group_index]
    pairs = jnp.stack([labels[:TOK_DEV], labels[TOK_DEV:]], axis=1)
    row_order = jax.random.permutation(key_rows, TOK_DEV).astype(jnp.int32)
    pairs = pairs[row_order]
    flips = jax.random.randint(key_flip, (TOK_DEV,), 0, 2)
    pairs = jnp.where(flips[:, None] == 1, pairs[:, ::-1], pairs)
    return pairs.astype(jnp.int32)


def draw_expert_ids(key, part):
    key = jax.random.fold_in(key, 11)
    blocks = TOKENS // TOK_DEV
    block_keys = jax.random.split(key, blocks)
    pairs = jax.vmap(route_block)(block_keys)
    return pairs.reshape(TOKENS, 2).astype(jnp.int32)


def levels(rng, shape, cuts, least, largest):
    level, own = 1.0, jax.random.fold_in(rng, 6)
    for position, parts in cuts:
        draws = jnp.exp(jax.random.uniform(jax.random.fold_in(own, position), (parts,), jnp.float32, least / len(cuts), largest / len(cuts)))
        level = level * jnp.repeat(draws, shape[position] // parts).reshape([-1 if axis == position else 1 for axis in range(len(shape))])
    return level


def centred(key, shape, deviation, most, cuts=(), kind=jnp.bfloat16):
    values = jax.random.normal(key, shape, jnp.float32) * deviation
    if len(cuts) > 0:
        values = levels(key, shape, cuts, -0.22, 0.18) * values
    return jnp.clip(values, min=-most, max=most).astype(kind)


def setup_inputs(seed: int = 0, part: int = 0) -> dict:
    splits = jax.random.split(jax.random.key(seed), 7)
    own_keys = jax.random.split(jax.random.fold_in(splits[6], part), 7)
    return {
        "tokens": centred(own_keys[0], (TOKENS, D), 1.0, 6.0, ((0, 4),)),
        "expert_ids": draw_expert_ids(jax.random.fold_in(jax.random.fold_in(splits[6], part), 71), part),
        "route_logits": centred(own_keys[2], (TOKENS, 2), 0.5, 3.0, ((0, 4),), jnp.float32),
        "w_gate": centred(splits[3], (EXP_WIN, FF, D), D ** -0.5, 0.125, ((1, 4),)),
        "w_up": centred(splits[4], (EXP_WIN, FF, D), D ** -0.5, 0.125, ((1, 4),)),
        "w_down": centred(splits[5], (EXP_WIN, FF, D), FF ** -0.5, 0.0625, ((1, 4),)),
    }


def reference(tokens, expert_ids, route_logits, w_gate, w_up, w_down):
    route_probs = jax.nn.softmax(route_logits.astype(jnp.float32), axis=-1).astype(jnp.bfloat16)
    probs_wide = route_probs.astype(jnp.float32)
    limit = N_ET * CAP
    block_units = FF // N_ET
    result = jnp.zeros((tokens.shape[0], tokens.shape[1]), jnp.float32)
    for expert in range(EXP_WIN):
        chosen = expert_ids == expert
        combine = jnp.sum(jnp.where(chosen, probs_wide, jnp.float32(0.0)), axis=-1)
        routed = jnp.any(chosen, axis=-1)
        routed_count = jnp.sum(routed.astype(jnp.int32))
        picks = jnp.nonzero(routed, size=limit, fill_value=0)[0].astype(jnp.int32)
        in_use = jnp.arange(limit, dtype=jnp.int32) < routed_count
        slot_weight = jnp.where(in_use, combine[picks], jnp.float32(0.0))
        picked = tokens[picks].astype(jnp.float32)
        gate_act = jnp.dot(picked, w_gate[expert].astype(jnp.float32).T, precision=lax.Precision.HIGHEST)
        up_act = jnp.dot(picked, w_up[expert].astype(jnp.float32).T, precision=lax.Precision.HIGHEST)
        hidden = (jax.nn.silu(gate_act) * up_act).astype(jnp.bfloat16)
        hidden = lax.optimization_barrier(hidden).astype(jnp.float32)
        hidden_blocks = hidden.reshape(limit, N_ET, block_units)
        down_blocks = w_down[expert].astype(jnp.float32).reshape(N_ET, block_units, tokens.shape[1])
        block_out = jnp.einsum("lnf,nfd->lnd", hidden_blocks, down_blocks, precision=lax.Precision.HIGHEST)
        term = (slot_weight[:, None, None] * block_out).astype(jnp.bfloat16)
        term = lax.optimization_barrier(term).astype(jnp.float32)
        result = result.at[picks].add(jnp.sum(term, axis=1))
    return result.astype(jnp.bfloat16)
```

```python
import functools

import jax
import jax.numpy as jnp
from jax import lax
from jax.experimental import pallas as pl
from jax.experimental.pallas import tpu as pltpu
from jax.sharding import PartitionSpec as P

EXP_WIN = 2
CAP = 48
CHUNKS = ((0, 16), (0, 32), (1, 32), (1, 16))
F_TILE = 256
D_TILE = 512
MESH = pl.DeviceIdType.MESH


def chunk_starts():
    starts, seen = [], 0
    for _, rows in CHUNKS:
        starts.append(seen)
        seen += rows
    return starts


def routing(ids, logits):
    rows, slots = ids.shape[1], EXP_WIN * CAP
    low, high = logits[0:1, :], logits[1:2, :]
    top = jnp.maximum(low, high)
    exp_low, exp_high = jnp.exp(low - top), jnp.exp(high - top)
    total = exp_low + exp_high
    prob_low = (exp_low / total).astype(jnp.bfloat16).astype(jnp.float32)
    prob_high = (exp_high / total).astype(jnp.bfloat16).astype(jnp.float32)
    slot = lax.broadcasted_iota(jnp.int32, (slots, rows), 0)
    expert = jnp.where(slot >= CAP, 1, 0)
    in_low, in_high = ids[0:1, :] == expert, ids[1:2, :] == expert
    weight = jnp.where(in_low, prob_low, 0.0) + jnp.where(in_high, prob_high, 0.0)
    routed = jnp.where(in_low, 1.0, 0.0) + jnp.where(in_high, 1.0, 0.0)
    upper = lax.broadcasted_iota(jnp.int32, (rows, rows), 0) <= lax.broadcasted_iota(jnp.int32, (rows, rows), 1)
    ranking = jnp.dot(
        routed.astype(jnp.bfloat16), jnp.where(upper, 1.0, 0.0).astype(jnp.bfloat16), preferred_element_type=jnp.float32
    )
    place = (slot - CAP * expert + 1).astype(jnp.float32)
    selected = jnp.where(ranking == place, routed, 0.0)
    return selected.astype(jnp.bfloat16), (selected * weight).astype(jnp.bfloat16)


def kernel(n, tokens, ids, logits, w_gate, w_up, w_down, out, *scratch):
    count = len(CHUNKS)
    rows_of = scratch[0:count]
    term_of = scratch[count : 2 * count]
    right_of = scratch[2 * count : 3 * count]
    left_of = scratch[3 * count : 4 * count]
    gate, up, down, hidden, own, weighted, load_sem, ag_send, ag_recv, rs_send, rs_recv = scratch[4 * count :]
    p = lax.axis_index("et")
    features = tokens.shape[1]
    units = gate.shape[1]
    f_tile = F_TILE if units % F_TILE == 0 else units
    f_steps, d_steps = units // f_tile, features // D_TILE
    starts = chunk_starts()
    has_left, has_right = p > 0, p < n - 1

    def load(index, expert):
        source, held = ((w_gate, gate), (w_up, up), (w_down, down))[index]
        return pltpu.make_async_copy(source.at[expert], held.at[expert], load_sem.at[index, expert])

    for index in range(3):
        load(index, 0).start()

    barrier = pltpu.get_barrier_semaphore()

    @pl.when(has_left)
    def _():
        pl.semaphore_signal(barrier, inc=1, device_id={"et": p - 1}, device_id_type=MESH)

    @pl.when(has_right)
    def _():
        pl.semaphore_signal(barrier, inc=1, device_id={"et": p + 1}, device_id_type=MESH)

    plain, scaled = routing(ids[...], logits[...])
    weighted[...] = scaled
    for part in range(d_steps):
        columns = pl.ds(part * D_TILE, D_TILE)
        picked = jnp.dot(plain, tokens[:, columns], preferred_element_type=jnp.float32).astype(jnp.bfloat16)
        for c, (_, size) in enumerate(CHUNKS):
            rows_of[c][p, :, columns] = picked[starts[c] : starts[c] + size]

    pl.semaphore_wait(barrier, jnp.where(has_left & has_right, 2, 1))

    def ag_right(c, k):
        return pltpu.make_async_remote_copy(
            src_ref=rows_of[c].at[p - k],
            dst_ref=rows_of[c].at[p - k],
            send_sem=ag_send.at[0, c, k],
            recv_sem=ag_recv.at[0, c, k + 1],
            device_id={"et": p + 1},
            device_id_type=MESH,
        )

    def ag_left(c, k):
        return pltpu.make_async_remote_copy(
            src_ref=rows_of[c].at[p + k],
            dst_ref=rows_of[c].at[p + k],
            send_sem=ag_send.at[1, c, k],
            recv_sem=ag_recv.at[1, c, k + 1],
            device_id={"et": p - 1},
            device_id_type=MESH,
        )

    def ag_wait(c, k):
        @pl.when(p - k >= 0)
        def _():
            pltpu.make_async_remote_copy(
                src_ref=rows_of[c].at[p - k],
                dst_ref=rows_of[c].at[p - k],
                send_sem=ag_send.at[0, c, k - 1],
                recv_sem=ag_recv.at[0, c, k],
                device_id={"et": p - 1},
                device_id_type=MESH,
            ).wait_recv()

        @pl.when(p + k <= n - 1)
        def _():
            pltpu.make_async_remote_copy(
                src_ref=rows_of[c].at[p + k],
                dst_ref=rows_of[c].at[p + k],
                send_sem=ag_send.at[1, c, k - 1],
                recv_sem=ag_recv.at[1, c, k],
                device_id={"et": p + 1},
                device_id_type=MESH,
            ).wait_recv()

    def ag_each(c, k, act):
        @pl.when((p - k >= 0) & has_right)
        def _():
            act(ag_right(c, k))

        @pl.when((p + k <= n - 1) & has_left)
        def _():
            act(ag_left(c, k))

    def gather(c, k):
        if k > 0:
            ag_wait(c, k)
        if k < n - 1:
            ag_each(c, k, lambda copy: copy.start())

    def rs_copy(c, k, way):
        held = (right_of, left_of)[way][c]
        return pltpu.make_async_remote_copy(
            src_ref=held.at[k],
            dst_ref=held.at[k - 1],
            send_sem=rs_send.at[way, c, k],
            recv_sem=rs_recv.at[way, c, k - 1],
            device_id={"et": p + 1 if way == 0 else p - 1},
            device_id_type=MESH,
        )

    def rs_wait(c, k, way):
        held = (right_of, left_of)[way][c]
        pltpu.make_async_remote_copy(
            src_ref=held.at[k + 1],
            dst_ref=held.at[k],
            send_sem=rs_send.at[way, c, k + 1],
            recv_sem=rs_recv.at[way, c, k],
            device_id={"et": p - 1 if way == 0 else p + 1},
            device_id_type=MESH,
        ).wait_recv()

    def rs_step(c, k):
        for way in range(2):
            held = (right_of, left_of)[way][c]
            target = p + k if way == 0 else p - k
            exists = target <= n - 1 if way == 0 else target >= 0
            behind = has_left if way == 0 else has_right
            if k < n - 1:

                @pl.when(exists & behind)
                def _():
                    rs_wait(c, k, way)
                    held[k] = (held[k].astype(jnp.float32) + term_of[c][target].astype(jnp.float32)).astype(jnp.bfloat16)

            @pl.when(exists & jnp.logical_not(behind))
            def _():
                held[k] = term_of[c][target]

            @pl.when(exists)
            def _():
                rs_copy(c, k, way).start()

    def gate_up(c, first, last):
        expert, size = CHUNKS[c]
        m = n * size

        @pl.loop(first, last)
        def _(i):
            at = pl.ds(pl.multiple_of(i * f_tile, f_tile), f_tile)
            x = rows_of[c][...].reshape(m, features)
            dims = (((1,), (1,)), ((), ()))
            g = lax.dot_general(x, gate[expert, at, :], dims, preferred_element_type=jnp.float32)
            u = lax.dot_general(x, up[expert, at, :], dims, preferred_element_type=jnp.float32)
            hidden[0:m, at] = (g / (1.0 + jnp.exp(-g)) * u).astype(jnp.bfloat16)

    def project(c, first, last):
        expert, size = CHUNKS[c]
        m = n * size

        @pl.loop(first, last)
        def _(j):
            at = pl.ds(pl.multiple_of(j * D_TILE, D_TILE), D_TILE)
            y = jnp.dot(hidden[0:m, :], down[expert, :, at], preferred_element_type=jnp.float32)
            term_of[c][:, :, at] = y.astype(jnp.bfloat16).reshape(n, size, D_TILE)

    for k in range(n):
        gather(0, k)
        if k == n - 2 and count > 1:
            gather(1, 0)

    for c, (expert, size) in enumerate(CHUNKS):
        first_use = c == 0 or CHUNKS[c - 1][0] != expert
        pieces = []
        half = f_steps // 2
        if half > 0:
            pieces.append(functools.partial(gate_up, c, 0, half))
        pieces.append(functools.partial(gate_up, c, half, f_steps))
        pieces.append(functools.partial(project, c, 0, d_steps // 2))
        pieces.append(functools.partial(project, c, d_steps // 2, d_steps))
        services = []
        for k in range(1, n - 1):
            if c + 1 < count:
                services.append(functools.partial(gather, c + 1, k))
            if c > 0:
                services.append(functools.partial(rs_step, c - 1, n - 1 - k))
        if c + 2 < count:
            services.append(functools.partial(gather, c + 2, 0))
        if first_use:
            load(0, expert).wait()
            load(1, expert).wait()
        if c == 0:
            for index in range(3):
                load(index, 1).start()
        done = 0
        for i, piece in enumerate(pieces):
            if first_use and i == len(pieces) - 2:
                load(2, expert).wait()
            piece()
            upto = (i + 1) * len(services) // len(pieces)
            for service in services[done:upto]:
                service()
            done = upto
        rs_step(c, n - 1)
        if c + 1 < count:
            gather(c + 1, n - 1)
    for k in range(n - 2, 0, -1):
        rs_step(count - 1, k)

    for c, (_, size) in enumerate(CHUNKS):
        at = pl.ds(starts[c], size)
        own[at, :] = term_of[c][p]

        @pl.when(has_left)
        def _():
            rs_wait(c, 0, 0)

        @pl.when(has_right)
        def _():
            rs_wait(c, 0, 1)

        @pl.when(has_left & has_right)
        def _():
            total = right_of[c][0].astype(jnp.float32) + left_of[c][0].astype(jnp.float32)
            own[at, :] = (total + term_of[c][p].astype(jnp.float32)).astype(jnp.bfloat16)

        @pl.when(has_left & jnp.logical_not(has_right))
        def _():
            own[at, :] = (right_of[c][0].astype(jnp.float32) + term_of[c][p].astype(jnp.float32)).astype(jnp.bfloat16)

        @pl.when(has_right & jnp.logical_not(has_left))
        def _():
            own[at, :] = (left_of[c][0].astype(jnp.float32) + term_of[c][p].astype(jnp.float32)).astype(jnp.bfloat16)

    for part in range(d_steps):
        columns = pl.ds(part * D_TILE, D_TILE)
        mixed = lax.dot_general(
            weighted[...], own[:, columns], (((0,), (0,)), ((), ())), preferred_element_type=jnp.float32
        )
        out[:, columns] = mixed.astype(jnp.bfloat16)

    for c in range(count):
        for k in range(n - 1):
            ag_each(c, k, lambda copy: copy.wait_send())
        for k in range(1, n):

            @pl.when(p + k <= n - 1)
            def _():
                rs_copy(c, k, 0).wait_send()

            @pl.when(p - k >= 0)
            def _():
                rs_copy(c, k, 1).wait_send()


def body(n, tokens, expert_ids, route_logits, w_gate, w_up, w_down):
    count, features, units = len(CHUNKS), tokens.shape[1], w_gate.shape[1]
    most = max(size for _, size in CHUNKS)
    per_chunk = [pltpu.VMEM((n, size, features), jnp.bfloat16) for _, size in CHUNKS]
    vmem = pl.BlockSpec(memory_space=pltpu.VMEM)
    hbm = pl.BlockSpec(memory_space=pl.ANY)
    weights = pltpu.VMEM((EXP_WIN, units, features), jnp.bfloat16)
    return pl.pallas_call(
        functools.partial(kernel, n),
        out_shape=jax.ShapeDtypeStruct(tokens.shape, jnp.bfloat16),
        in_specs=[vmem, vmem, vmem, hbm, hbm, hbm],
        out_specs=vmem,
        scratch_shapes=per_chunk * 4
        + [
            weights,
            weights,
            weights,
            pltpu.VMEM((n * most, units), jnp.bfloat16),
            pltpu.VMEM((EXP_WIN * CAP, features), jnp.bfloat16),
            pltpu.VMEM((EXP_WIN * CAP, tokens.shape[0]), jnp.bfloat16),
            pltpu.SemaphoreType.DMA((3, EXP_WIN)),
            pltpu.SemaphoreType.DMA((2, count, n)),
            pltpu.SemaphoreType.DMA((2, count, n)),
            pltpu.SemaphoreType.DMA((2, count, n)),
            pltpu.SemaphoreType.DMA((2, count, n)),
        ],
        compiler_params=pltpu.CompilerParams(collective_id=0, has_side_effects=True, vmem_limit_bytes=60 * 2**20),
    )(tokens, expert_ids.T, route_logits.T, w_gate, w_up, w_down)


def solution(mesh):
    in_specs = (
        P(("rep", "et"), None),
        P(("rep", "et"), None),
        P(("rep", "et"), None),
        P(None, "et", None),
        P(None, "et", None),
        P(None, "et", None),
    )
    out_specs = P(("rep", "et"), None)
    return jax.shard_map(
        functools.partial(body, mesh.shape["et"]), mesh=mesh, in_specs=in_specs, out_specs=out_specs, check_vma=False
    )
```

```python
import functools

import jax
import jax.numpy as jnp
from jax import lax
from jax.experimental import pallas as pl
from jax.experimental.pallas import tpu as pltpu
from jax.sharding import PartitionSpec as P

EXP_WIN = 2
CAP = 48
CHUNKS = ((0, 48), (1, 48))
F_TILE = 256
D_TILE = 512
MESH = pl.DeviceIdType.MESH


def chunk_starts():
    starts, seen = [], 0
    for _, rows in CHUNKS:
        starts.append(seen)
        seen += rows
    return starts


def routing(ids, logits):
    rows, slots = ids.shape[1], EXP_WIN * CAP
    low, high = logits[0:1, :], logits[1:2, :]
    top = jnp.maximum(low, high)
    exp_low, exp_high = jnp.exp(low - top), jnp.exp(high - top)
    total = exp_low + exp_high
    prob_low = (exp_low / total).astype(jnp.bfloat16).astype(jnp.float32)
    prob_high = (exp_high / total).astype(jnp.bfloat16).astype(jnp.float32)
    slot = lax.broadcasted_iota(jnp.int32, (slots, rows), 0)
    expert = jnp.where(slot >= CAP, 1, 0)
    in_low, in_high = ids[0:1, :] == expert, ids[1:2, :] == expert
    weight = jnp.where(in_low, prob_low, 0.0) + jnp.where(in_high, prob_high, 0.0)
    routed = jnp.where(in_low, 1.0, 0.0) + jnp.where(in_high, 1.0, 0.0)
    upper = lax.broadcasted_iota(jnp.int32, (rows, rows), 0) <= lax.broadcasted_iota(jnp.int32, (rows, rows), 1)
    ranking = jnp.dot(
        routed.astype(jnp.bfloat16), jnp.where(upper, 1.0, 0.0).astype(jnp.bfloat16), preferred_element_type=jnp.float32
    )
    place = (slot - CAP * expert + 1).astype(jnp.float32)
    selected = jnp.where(ranking == place, routed, 0.0)
    return selected.astype(jnp.bfloat16), (selected * weight).astype(jnp.bfloat16)


def kernel(n, tokens, ids, logits, w_gate, w_up, w_down, out, *scratch):
    count = len(CHUNKS)
    rows_of = scratch[0:count]
    term_of = scratch[count : 2 * count]
    right_of = scratch[2 * count : 3 * count]
    left_of = scratch[3 * count : 4 * count]
    gate, up, down, hidden, own, weighted, load_sem, ag_send, ag_recv, rs_send, rs_recv = scratch[4 * count :]
    p = lax.axis_index("et")
    features = tokens.shape[1]
    units = gate.shape[1]
    f_tile = F_TILE if units % F_TILE == 0 else units
    f_steps, d_steps = units // f_tile, features // D_TILE
    starts = chunk_starts()
    has_left, has_right = p > 0, p < n - 1

    def load(index, expert):
        source, held = ((w_gate, gate), (w_up, up), (w_down, down))[index]
        return pltpu.make_async_copy(source.at[expert], held.at[expert], load_sem.at[index, expert])

    for index in range(3):
        load(index, 0).start()

    barrier = pltpu.get_barrier_semaphore()

    @pl.when(has_left)
    def _():
        pl.semaphore_signal(barrier, inc=1, device_id={"et": p - 1}, device_id_type=MESH)

    @pl.when(has_right)
    def _():
        pl.semaphore_signal(barrier, inc=1, device_id={"et": p + 1}, device_id_type=MESH)

    plain, scaled = routing(ids[...], logits[...])
    weighted[...] = scaled
    for part in range(d_steps):
        columns = pl.ds(part * D_TILE, D_TILE)
        picked = jnp.dot(plain, tokens[:, columns], preferred_element_type=jnp.float32).astype(jnp.bfloat16)
        for c, (_, size) in enumerate(CHUNKS):
            rows_of[c][p, :, columns] = picked[starts[c] : starts[c] + size]

    pl.semaphore_wait(barrier, jnp.where(has_left & has_right, 2, 1))

    def ag_right(c, k):
        return pltpu.make_async_remote_copy(
            src_ref=rows_of[c].at[p - k],
            dst_ref=rows_of[c].at[p - k],
            send_sem=ag_send.at[0, c, k],
            recv_sem=ag_recv.at[0, c, k + 1],
            device_id={"et": p + 1},
            device_id_type=MESH,
        )

    def ag_left(c, k):
        return pltpu.make_async_remote_copy(
            src_ref=rows_of[c].at[p + k],
            dst_ref=rows_of[c].at[p + k],
            send_sem=ag_send.at[1, c, k],
            recv_sem=ag_recv.at[1, c, k + 1],
            device_id={"et": p - 1},
            device_id_type=MESH,
        )

    def ag_wait(c, k):
        @pl.when(p - k >= 0)
        def _():
            pltpu.make_async_remote_copy(
                src_ref=rows_of[c].at[p - k],
                dst_ref=rows_of[c].at[p - k],
                send_sem=ag_send.at[0, c, k - 1],
                recv_sem=ag_recv.at[0, c, k],
                device_id={"et": p - 1},
                device_id_type=MESH,
            ).wait_recv()

        @pl.when(p + k <= n - 1)
        def _():
            pltpu.make_async_remote_copy(
                src_ref=rows_of[c].at[p + k],
                dst_ref=rows_of[c].at[p + k],
                send_sem=ag_send.at[1, c, k - 1],
                recv_sem=ag_recv.at[1, c, k],
                device_id={"et": p + 1},
                device_id_type=MESH,
            ).wait_recv()

    def ag_each(c, k, act):
        @pl.when((p - k >= 0) & has_right)
        def _():
            act(ag_right(c, k))

        @pl.when((p + k <= n - 1) & has_left)
        def _():
            act(ag_left(c, k))

    def gather(c, k):
        if k > 0:
            ag_wait(c, k)
        if k < n - 1:
            ag_each(c, k, lambda copy: copy.start())

    def rs_copy(c, k, way):
        held = (right_of, left_of)[way][c]
        return pltpu.make_async_remote_copy(
            src_ref=held.at[k],
            dst_ref=held.at[k - 1],
            send_sem=rs_send.at[way, c, k],
            recv_sem=rs_recv.at[way, c, k - 1],
            device_id={"et": p + 1 if way == 0 else p - 1},
            device_id_type=MESH,
        )

    def rs_wait(c, k, way):
        held = (right_of, left_of)[way][c]
        pltpu.make_async_remote_copy(
            src_ref=held.at[k + 1],
            dst_ref=held.at[k],
            send_sem=rs_send.at[way, c, k + 1],
            recv_sem=rs_recv.at[way, c, k],
            device_id={"et": p - 1 if way == 0 else p + 1},
            device_id_type=MESH,
        ).wait_recv()

    def rs_step(c, k):
        for way in range(2):
            held = (right_of, left_of)[way][c]
            target = p + k if way == 0 else p - k
            exists = target <= n - 1 if way == 0 else target >= 0
            behind = has_left if way == 0 else has_right
            if k < n - 1:

                @pl.when(exists & behind)
                def _():
                    rs_wait(c, k, way)
                    held[k] = (held[k].astype(jnp.float32) + term_of[c][target].astype(jnp.float32)).astype(jnp.bfloat16)

            @pl.when(exists & jnp.logical_not(behind))
            def _():
                held[k] = term_of[c][target]

            @pl.when(exists)
            def _():
                rs_copy(c, k, way).start()

    def gate_up(c, first, last):
        expert, size = CHUNKS[c]
        m = n * size

        @pl.loop(first, last)
        def _(i):
            at = pl.ds(pl.multiple_of(i * f_tile, f_tile), f_tile)
            x = rows_of[c][...].reshape(m, features)
            dims = (((1,), (1,)), ((), ()))
            g = lax.dot_general(x, gate[expert, at, :], dims, preferred_element_type=jnp.float32)
            u = lax.dot_general(x, up[expert, at, :], dims, preferred_element_type=jnp.float32)
            hidden[0:m, at] = (g / (1.0 + jnp.exp(-g)) * u).astype(jnp.bfloat16)

    def project(c, first, last):
        expert, size = CHUNKS[c]
        m = n * size

        @pl.loop(first, last)
        def _(j):
            at = pl.ds(pl.multiple_of(j * D_TILE, D_TILE), D_TILE)
            y = jnp.dot(hidden[0:m, :], down[expert, :, at], preferred_element_type=jnp.float32)
            term_of[c][:, :, at] = y.astype(jnp.bfloat16).reshape(n, size, D_TILE)

    for k in range(n):
        gather(0, k)
        if k == n - 2 and count > 1:
            gather(1, 0)

    for c, (expert, size) in enumerate(CHUNKS):
        first_use = c == 0 or CHUNKS[c - 1][0] != expert
        pieces = []
        half = f_steps // 2
        if half > 0:
            pieces.append(functools.partial(gate_up, c, 0, half))
        pieces.append(functools.partial(gate_up, c, half, f_steps))
        pieces.append(functools.partial(project, c, 0, d_steps // 2))
        pieces.append(functools.partial(project, c, d_steps // 2, d_steps))
        services = []
        for k in range(1, n - 1):
            if c + 1 < count:
                services.append(functools.partial(gather, c + 1, k))
            if c > 0:
                services.append(functools.partial(rs_step, c - 1, n - 1 - k))
        if c + 2 < count:
            services.append(functools.partial(gather, c + 2, 0))
        if first_use:
            load(0, expert).wait()
            load(1, expert).wait()
        if c == 0:
            for index in range(3):
                load(index, 1).start()
        done = 0
        for i, piece in enumerate(pieces):
            if first_use and i == len(pieces) - 2:
                load(2, expert).wait()
            piece()
            upto = (i + 1) * len(services) // len(pieces)
            for service in services[done:upto]:
                service()
            done = upto
        rs_step(c, n - 1)
        if c + 1 < count:
            gather(c + 1, n - 1)
    for k in range(n - 2, 0, -1):
        rs_step(count - 1, k)

    for c, (_, size) in enumerate(CHUNKS):
        at = pl.ds(starts[c], size)
        own[at, :] = term_of[c][p]

        @pl.when(has_left)
        def _():
            rs_wait(c, 0, 0)

        @pl.when(has_right)
        def _():
            rs_wait(c, 0, 1)

        @pl.when(has_left & has_right)
        def _():
            total = right_of[c][0].astype(jnp.float32) + left_of[c][0].astype(jnp.float32)
            own[at, :] = (total + term_of[c][p].astype(jnp.float32)).astype(jnp.bfloat16)

        @pl.when(has_left & jnp.logical_not(has_right))
        def _():
            own[at, :] = (right_of[c][0].astype(jnp.float32) + term_of[c][p].astype(jnp.float32)).astype(jnp.bfloat16)

        @pl.when(has_right & jnp.logical_not(has_left))
        def _():
            own[at, :] = (left_of[c][0].astype(jnp.float32) + term_of[c][p].astype(jnp.float32)).astype(jnp.bfloat16)

    for part in range(d_steps):
        columns = pl.ds(part * D_TILE, D_TILE)
        mixed = lax.dot_general(
            weighted[...], own[:, columns], (((0,), (0,)), ((), ())), preferred_element_type=jnp.float32
        )
        out[:, columns] = mixed.astype(jnp.bfloat16)

    for c in range(count):
        for k in range(n - 1):
            ag_each(c, k, lambda copy: copy.wait_send())
        for k in range(1, n):

            @pl.when(p + k <= n - 1)
            def _():
                rs_copy(c, k, 0).wait_send()

            @pl.when(p - k >= 0)
            def _():
                rs_copy(c, k, 1).wait_send()


def body(n, tokens, expert_ids, route_logits, w_gate, w_up, w_down):
    count, features, units = len(CHUNKS), tokens.shape[1], w_gate.shape[1]
    most = max(size for _, size in CHUNKS)
    per_chunk = [pltpu.VMEM((n, size, features), jnp.bfloat16) for _, size in CHUNKS]
    vmem = pl.BlockSpec(memory_space=pltpu.VMEM)
    hbm = pl.BlockSpec(memory_space=pl.ANY)
    weights = pltpu.VMEM((EXP_WIN, units, features), jnp.bfloat16)
    return pl.pallas_call(
        functools.partial(kernel, n),
        out_shape=jax.ShapeDtypeStruct(tokens.shape, jnp.bfloat16),
        in_specs=[vmem, vmem, vmem, hbm, hbm, hbm],
        out_specs=vmem,
        scratch_shapes=per_chunk * 4
        + [
            weights,
            weights,
            weights,
            pltpu.VMEM((n * most, units), jnp.bfloat16),
            pltpu.VMEM((EXP_WIN * CAP, features), jnp.bfloat16),
            pltpu.VMEM((EXP_WIN * CAP, tokens.shape[0]), jnp.bfloat16),
            pltpu.SemaphoreType.DMA((3, EXP_WIN)),
            pltpu.SemaphoreType.DMA((2, count, n)),
            pltpu.SemaphoreType.DMA((2, count, n)),
            pltpu.SemaphoreType.DMA((2, count, n)),
            pltpu.SemaphoreType.DMA((2, count, n)),
        ],
        compiler_params=pltpu.CompilerParams(collective_id=0, has_side_effects=True, vmem_limit_bytes=60 * 2**20),
    )(tokens, expert_ids.T, route_logits.T, w_gate, w_up, w_down)


def solution(mesh):
    in_specs = (
        P(("rep", "et"), None),
        P(("rep", "et"), None),
        P(("rep", "et"), None),
        P(None, "et", None),
        P(None, "et", None),
        P(None, "et", None),
    )
    out_specs = P(("rep", "et"), None)
    return jax.shard_map(
        functools.partial(body, mesh.shape["et"]), mesh=mesh, in_specs=in_specs, out_specs=out_specs, check_vma=False
    )
```

```python
import functools

import jax
import jax.numpy as jnp
from jax import lax
from jax.experimental import pallas as pl
from jax.experimental.pallas import tpu as pltpu
from jax.sharding import PartitionSpec as P

EXP_WIN = 2
CAP = 48
CHUNKS = ((0, 48), (1, 48))
F_TILE = 256
D_TILE = 512
MESH = pl.DeviceIdType.MESH


def chunk_starts():
    starts, seen = [], 0
    for _, rows in CHUNKS:
        starts.append(seen)
        seen += rows
    return starts


def routing(ids, logits):
    rows, slots = ids.shape[1], EXP_WIN * CAP
    low, high = logits[0:1, :], logits[1:2, :]
    top = jnp.maximum(low, high)
    exp_low, exp_high = jnp.exp(low - top), jnp.exp(high - top)
    total = exp_low + exp_high
    prob_low = (exp_low / total).astype(jnp.bfloat16).astype(jnp.float32)
    prob_high = (exp_high / total).astype(jnp.bfloat16).astype(jnp.float32)
    slot = lax.broadcasted_iota(jnp.int32, (slots, rows), 0)
    expert = jnp.where(slot >= CAP, 1, 0)
    in_low, in_high = ids[0:1, :] == expert, ids[1:2, :] == expert
    weight = jnp.where(in_low, prob_low, 0.0) + jnp.where(in_high, prob_high, 0.0)
    routed = jnp.where(in_low, 1.0, 0.0) + jnp.where(in_high, 1.0, 0.0)
    upper = lax.broadcasted_iota(jnp.int32, (rows, rows), 0) <= lax.broadcasted_iota(jnp.int32, (rows, rows), 1)
    ranking = jnp.dot(
        routed.astype(jnp.bfloat16), jnp.where(upper, 1.0, 0.0).astype(jnp.bfloat16), preferred_element_type=jnp.float32
    )
    place = (slot - CAP * expert + 1).astype(jnp.float32)
    selected = jnp.where(ranking == place, routed, 0.0)
    return selected.astype(jnp.bfloat16), (selected * weight).astype(jnp.bfloat16)


def kernel(n, tokens, ids, logits, w_gate, w_up, w_down, out, *scratch):
    count = len(CHUNKS)
    rows_of = scratch[0:count]
    term_of = scratch[count : 2 * count]
    right_of = scratch[2 * count : 3 * count]
    left_of = scratch[3 * count : 4 * count]
    gate, up, down, turned, hidden, own, weighted, load_sem, ag_send, ag_recv, rs_send, rs_recv = scratch[4 * count :]
    p = lax.axis_index("et")
    features = tokens.shape[1]
    units = gate.shape[1]
    f_tile = F_TILE if units % F_TILE == 0 else units
    f_steps, d_steps = units // f_tile, features // D_TILE
    starts = chunk_starts()
    has_left, has_right = p > 0, p < n - 1

    def load(index, expert):
        source, held = ((w_gate, gate), (w_up, up), (w_down, down))[index]
        return pltpu.make_async_copy(source.at[expert], held.at[expert], load_sem.at[index, expert])

    for index in range(3):
        load(index, 0).start()

    barrier = pltpu.get_barrier_semaphore()

    @pl.when(has_left)
    def _():
        pl.semaphore_signal(barrier, inc=1, device_id={"et": p - 1}, device_id_type=MESH)

    @pl.when(has_right)
    def _():
        pl.semaphore_signal(barrier, inc=1, device_id={"et": p + 1}, device_id_type=MESH)

    plain, scaled = routing(ids[...], logits[...])
    weighted[...] = scaled
    for part in range(d_steps):
        columns = pl.ds(part * D_TILE, D_TILE)
        picked = jnp.dot(plain, tokens[:, columns], preferred_element_type=jnp.float32).astype(jnp.bfloat16)
        for c, (_, size) in enumerate(CHUNKS):
            rows_of[c][p, :, columns] = picked[starts[c] : starts[c] + size]

    pl.semaphore_wait(barrier, jnp.where(has_left & has_right, 2, 1))

    def ag_right(c, k):
        return pltpu.make_async_remote_copy(
            src_ref=rows_of[c].at[p - k],
            dst_ref=rows_of[c].at[p - k],
            send_sem=ag_send.at[0, c, k],
            recv_sem=ag_recv.at[0, c, k + 1],
            device_id={"et": p + 1},
            device_id_type=MESH,
        )

    def ag_left(c, k):
        return pltpu.make_async_remote_copy(
            src_ref=rows_of[c].at[p + k],
            dst_ref=rows_of[c].at[p + k],
            send_sem=ag_send.at[1, c, k],
            recv_sem=ag_recv.at[1, c, k + 1],
            device_id={"et": p - 1},
            device_id_type=MESH,
        )

    def ag_wait(c, k):
        @pl.when(p - k >= 0)
        def _():
            pltpu.make_async_remote_copy(
                src_ref=rows_of[c].at[p - k],
                dst_ref=rows_of[c].at[p - k],
                send_sem=ag_send.at[0, c, k - 1],
                recv_sem=ag_recv.at[0, c, k],
                device_id={"et": p - 1},
                device_id_type=MESH,
            ).wait_recv()

        @pl.when(p + k <= n - 1)
        def _():
            pltpu.make_async_remote_copy(
                src_ref=rows_of[c].at[p + k],
                dst_ref=rows_of[c].at[p + k],
                send_sem=ag_send.at[1, c, k - 1],
                recv_sem=ag_recv.at[1, c, k],
                device_id={"et": p + 1},
                device_id_type=MESH,
            ).wait_recv()

    def ag_each(c, k, act):
        @pl.when((p - k >= 0) & has_right)
        def _():
            act(ag_right(c, k))

        @pl.when((p + k <= n - 1) & has_left)
        def _():
            act(ag_left(c, k))

    def gather(c, k):
        if k > 0:
            ag_wait(c, k)
        if k < n - 1:
            ag_each(c, k, lambda copy: copy.start())

    def rs_copy(c, k, way):
        held = (right_of, left_of)[way][c]
        return pltpu.make_async_remote_copy(
            src_ref=held.at[k],
            dst_ref=held.at[k - 1],
            send_sem=rs_send.at[way, c, k],
            recv_sem=rs_recv.at[way, c, k - 1],
            device_id={"et": p + 1 if way == 0 else p - 1},
            device_id_type=MESH,
        )

    def rs_wait(c, k, way):
        held = (right_of, left_of)[way][c]
        pltpu.make_async_remote_copy(
            src_ref=held.at[k + 1],
            dst_ref=held.at[k],
            send_sem=rs_send.at[way, c, k + 1],
            recv_sem=rs_recv.at[way, c, k],
            device_id={"et": p - 1 if way == 0 else p + 1},
            device_id_type=MESH,
        ).wait_recv()

    def rs_step(c, k):
        for way in range(2):
            held = (right_of, left_of)[way][c]
            target = p + k if way == 0 else p - k
            exists = target <= n - 1 if way == 0 else target >= 0
            behind = has_left if way == 0 else has_right
            if k < n - 1:

                @pl.when(exists & behind)
                def _():
                    rs_wait(c, k, way)
                    held[k] = (held[k].astype(jnp.float32) + term_of[c][target].astype(jnp.float32)).astype(jnp.bfloat16)

            @pl.when(exists & jnp.logical_not(behind))
            def _():
                held[k] = term_of[c][target]

            @pl.when(exists)
            def _():
                rs_copy(c, k, way).start()

    def turn(c):
        size = CHUNKS[c][1]
        m = n * size

        @pl.loop(0, d_steps)
        def _(j):
            at = pl.ds(pl.multiple_of(j * D_TILE, D_TILE), D_TILE)
            turned[at, 0:m] = rows_of[c][:, :, at].reshape(m, D_TILE).T

    def gate_up(c, first, last):
        expert, size = CHUNKS[c]
        m = n * size

        @pl.loop(first, last)
        def _(i):
            at = pl.ds(pl.multiple_of(i * f_tile, f_tile), f_tile)
            x = turned[:, 0:m]
            g = jnp.dot(gate[expert, at, :], x, preferred_element_type=jnp.float32)
            u = jnp.dot(up[expert, at, :], x, preferred_element_type=jnp.float32)
            hidden[0:m, at] = (g / (1.0 + jnp.exp(-g)) * u).T.astype(jnp.bfloat16)

    def project(c, first, last):
        expert, size = CHUNKS[c]
        m = n * size

        @pl.loop(first, last)
        def _(j):
            at = pl.ds(pl.multiple_of(j * D_TILE, D_TILE), D_TILE)
            y = jnp.dot(hidden[0:m, :], down[expert, :, at], preferred_element_type=jnp.float32)
            term_of[c][:, :, at] = y.astype(jnp.bfloat16).reshape(n, size, D_TILE)

    for k in range(n):
        gather(0, k)
        if k == n - 2 and count > 1:
            gather(1, 0)

    for c, (expert, size) in enumerate(CHUNKS):
        first_use = c == 0 or CHUNKS[c - 1][0] != expert
        turn(c)
        pieces = []
        half = f_steps // 2
        if half > 0:
            pieces.append(functools.partial(gate_up, c, 0, half))
        pieces.append(functools.partial(gate_up, c, half, f_steps))
        pieces.append(functools.partial(project, c, 0, d_steps // 2))
        pieces.append(functools.partial(project, c, d_steps // 2, d_steps))
        services = []
        for k in range(1, n - 1):
            if c + 1 < count:
                services.append(functools.partial(gather, c + 1, k))
            if c > 0:
                services.append(functools.partial(rs_step, c - 1, n - 1 - k))
        if c + 2 < count:
            services.append(functools.partial(gather, c + 2, 0))
        if first_use:
            load(0, expert).wait()
            load(1, expert).wait()
        if c == 0:
            for index in range(3):
                load(index, 1).start()
        done = 0
        for i, piece in enumerate(pieces):
            if first_use and i == len(pieces) - 2:
                load(2, expert).wait()
            piece()
            upto = (i + 1) * len(services) // len(pieces)
            for service in services[done:upto]:
                service()
            done = upto
        rs_step(c, n - 1)
        if c + 1 < count:
            gather(c + 1, n - 1)
    for k in range(n - 2, 0, -1):
        rs_step(count - 1, k)

    for c, (_, size) in enumerate(CHUNKS):
        at = pl.ds(starts[c], size)
        own[at, :] = term_of[c][p]

        @pl.when(has_left)
        def _():
            rs_wait(c, 0, 0)

        @pl.when(has_right)
        def _():
            rs_wait(c, 0, 1)

        @pl.when(has_left & has_right)
        def _():
            total = right_of[c][0].astype(jnp.float32) + left_of[c][0].astype(jnp.float32)
            own[at, :] = (total + term_of[c][p].astype(jnp.float32)).astype(jnp.bfloat16)

        @pl.when(has_left & jnp.logical_not(has_right))
        def _():
            own[at, :] = (right_of[c][0].astype(jnp.float32) + term_of[c][p].astype(jnp.float32)).astype(jnp.bfloat16)

        @pl.when(has_right & jnp.logical_not(has_left))
        def _():
            own[at, :] = (left_of[c][0].astype(jnp.float32) + term_of[c][p].astype(jnp.float32)).astype(jnp.bfloat16)

    for part in range(d_steps):
        columns = pl.ds(part * D_TILE, D_TILE)
        mixed = lax.dot_general(
            weighted[...], own[:, columns], (((0,), (0,)), ((), ())), preferred_element_type=jnp.float32
        )
        out[:, columns] = mixed.astype(jnp.bfloat16)

    for c in range(count):
        for k in range(n - 1):
            ag_each(c, k, lambda copy: copy.wait_send())
        for k in range(1, n):

            @pl.when(p + k <= n - 1)
            def _():
                rs_copy(c, k, 0).wait_send()

            @pl.when(p - k >= 0)
            def _():
                rs_copy(c, k, 1).wait_send()


def body(n, tokens, expert_ids, route_logits, w_gate, w_up, w_down):
    count, features, units = len(CHUNKS), tokens.shape[1], w_gate.shape[1]
    most = max(size for _, size in CHUNKS)
    per_chunk = [pltpu.VMEM((n, size, features), jnp.bfloat16) for _, size in CHUNKS]
    vmem = pl.BlockSpec(memory_space=pltpu.VMEM)
    hbm = pl.BlockSpec(memory_space=pl.ANY)
    weights = pltpu.VMEM((EXP_WIN, units, features), jnp.bfloat16)
    return pl.pallas_call(
        functools.partial(kernel, n),
        out_shape=jax.ShapeDtypeStruct(tokens.shape, jnp.bfloat16),
        in_specs=[vmem, vmem, vmem, hbm, hbm, hbm],
        out_specs=vmem,
        scratch_shapes=per_chunk * 4
        + [
            weights,
            weights,
            weights,
            pltpu.VMEM((features, n * most), jnp.bfloat16),
            pltpu.VMEM((n * most, units), jnp.bfloat16),
            pltpu.VMEM((EXP_WIN * CAP, features), jnp.bfloat16),
            pltpu.VMEM((EXP_WIN * CAP, tokens.shape[0]), jnp.bfloat16),
            pltpu.SemaphoreType.DMA((3, EXP_WIN)),
            pltpu.SemaphoreType.DMA((2, count, n)),
            pltpu.SemaphoreType.DMA((2, count, n)),
            pltpu.SemaphoreType.DMA((2, count, n)),
            pltpu.SemaphoreType.DMA((2, count, n)),
        ],
        compiler_params=pltpu.CompilerParams(collective_id=0, has_side_effects=True, vmem_limit_bytes=60 * 2**20),
    )(tokens, expert_ids.T, route_logits.T, w_gate, w_up, w_down)


def solution(mesh):
    in_specs = (
        P(("rep", "et"), None),
        P(("rep", "et"), None),
        P(("rep", "et"), None),
        P(None, "et", None),
        P(None, "et", None),
        P(None, "et", None),
    )
    out_specs = P(("rep", "et"), None)
    return jax.shard_map(
        functools.partial(body, mesh.shape["et"]), mesh=mesh, in_specs=in_specs, out_specs=out_specs, check_vma=False
    )
```

```python
import functools

import jax
import jax.numpy as jnp
from jax import lax
from jax.experimental import pallas as pl
from jax.experimental.pallas import tpu as pltpu
from jax.sharding import PartitionSpec as P

EXP_WIN = 2
CAP = 48
CHUNKS = ((0, 16), (0, 32), (1, 32), (1, 16))
UNIT = 16
F_TILE = 256
D_TILE = 512
MESH = pl.DeviceIdType.MESH


def chunk_starts():
    starts, seen = [], 0
    for _, rows in CHUNKS:
        starts.append(seen)
        seen += rows
    return starts


def routing(ids, logits):
    rows, slots = ids.shape[1], EXP_WIN * CAP
    low, high = logits[0:1, :], logits[1:2, :]
    top = jnp.maximum(low, high)
    exp_low, exp_high = jnp.exp(low - top), jnp.exp(high - top)
    total = exp_low + exp_high
    prob_low = (exp_low / total).astype(jnp.bfloat16).astype(jnp.float32)
    prob_high = (exp_high / total).astype(jnp.bfloat16).astype(jnp.float32)
    slot = lax.broadcasted_iota(jnp.int32, (slots, rows), 0)
    expert = jnp.where(slot >= CAP, 1, 0)
    in_low, in_high = ids[0:1, :] == expert, ids[1:2, :] == expert
    weight = jnp.where(in_low, prob_low, 0.0) + jnp.where(in_high, prob_high, 0.0)
    routed = jnp.where(in_low, 1.0, 0.0) + jnp.where(in_high, 1.0, 0.0)
    upper = lax.broadcasted_iota(jnp.int32, (rows, rows), 0) <= lax.broadcasted_iota(jnp.int32, (rows, rows), 1)
    ranking = jnp.dot(
        routed.astype(jnp.bfloat16), jnp.where(upper, 1.0, 0.0).astype(jnp.bfloat16), preferred_element_type=jnp.float32
    )
    place = (slot - CAP * expert + 1).astype(jnp.float32)
    selected = jnp.where(ranking == place, routed, 0.0)
    return selected.astype(jnp.bfloat16), (selected * weight).astype(jnp.bfloat16)


def kernel(n, tokens, ids, logits, w_gate, w_up, w_down, own, weighted, *scratch):
    count = len(CHUNKS)
    rows_of = scratch[0:count]
    term_of = scratch[count : 2 * count]
    right_of = scratch[2 * count : 3 * count]
    left_of = scratch[3 * count : 4 * count]
    gate, up, down, hidden, load_sem, ag_send, ag_recv, rs_send, rs_recv = scratch[4 * count :]
    p = lax.axis_index("et")
    features = tokens.shape[1]
    units = gate.shape[1]
    f_tile = F_TILE if units % F_TILE == 0 else units
    f_steps, d_steps = units // f_tile, features // D_TILE
    starts = chunk_starts()
    units_of = [(c, at) for c, (_, size) in enumerate(CHUNKS) for at in range(0, size, UNIT)]
    has_left, has_right = p > 0, p < n - 1

    def load(index, expert):
        source, held = ((w_gate, gate), (w_up, up), (w_down, down))[index]
        return pltpu.make_async_copy(source.at[expert], held.at[expert], load_sem.at[index, expert])

    for index in range(3):
        load(index, 0).start()

    barrier = pltpu.get_barrier_semaphore()

    @pl.when(has_left)
    def _():
        pl.semaphore_signal(barrier, inc=1, device_id={"et": p - 1}, device_id_type=MESH)

    @pl.when(has_right)
    def _():
        pl.semaphore_signal(barrier, inc=1, device_id={"et": p + 1}, device_id_type=MESH)

    plain, scaled = routing(ids[...], logits[...])
    weighted[...] = scaled
    for part in range(d_steps):
        columns = pl.ds(part * D_TILE, D_TILE)
        picked = jnp.dot(plain, tokens[:, columns], preferred_element_type=jnp.float32).astype(jnp.bfloat16)
        for c, (_, size) in enumerate(CHUNKS):
            rows_of[c][p, :, columns] = picked[starts[c] : starts[c] + size]

    pl.semaphore_wait(barrier, jnp.where(has_left & has_right, 2, 1))

    def ag_copy(u, k, way, arriving=False):
        c, at = units_of[u]
        source = p - k if way == 0 else p + k
        held = rows_of[c].at[source, pl.ds(at, UNIT)]
        step = k - 1 if arriving else k
        return pltpu.make_async_remote_copy(
            src_ref=held,
            dst_ref=held,
            send_sem=ag_send.at[way, u, step],
            recv_sem=ag_recv.at[way, u, step + 1],
            device_id={"et": p + 1 if (way == 0) != arriving else p - 1},
            device_id_type=MESH,
        )

    def ag_each(u, k, act):
        @pl.when((p - k >= 0) & has_right)
        def _():
            act(ag_copy(u, k, 0))

        @pl.when((p + k <= n - 1) & has_left)
        def _():
            act(ag_copy(u, k, 1))

    def gather(u, k):
        if k > 0:

            @pl.when(p - k >= 0)
            def _():
                ag_copy(u, k, 0, True).wait_recv()

            @pl.when(p + k <= n - 1)
            def _():
                ag_copy(u, k, 1, True).wait_recv()

        if k < n - 1:
            ag_each(u, k, lambda copy: copy.start())

    def rs_copy(c, k, way):
        held = (right_of, left_of)[way][c]
        return pltpu.make_async_remote_copy(
            src_ref=held.at[k],
            dst_ref=held.at[k - 1],
            send_sem=rs_send.at[way, c, k],
            recv_sem=rs_recv.at[way, c, k - 1],
            device_id={"et": p + 1 if way == 0 else p - 1},
            device_id_type=MESH,
        )

    def rs_wait(c, k, way):
        held = (right_of, left_of)[way][c]
        pltpu.make_async_remote_copy(
            src_ref=held.at[k + 1],
            dst_ref=held.at[k],
            send_sem=rs_send.at[way, c, k + 1],
            recv_sem=rs_recv.at[way, c, k],
            device_id={"et": p - 1 if way == 0 else p + 1},
            device_id_type=MESH,
        ).wait_recv()

    def rs_step(c, k):
        for way in range(2):
            held = (right_of, left_of)[way][c]
            target = p + k if way == 0 else p - k
            exists = target <= n - 1 if way == 0 else target >= 0
            behind = has_left if way == 0 else has_right
            if k < n - 1:

                @pl.when(exists & behind)
                def _():
                    rs_wait(c, k, way)
                    held[k] = (held[k].astype(jnp.float32) + term_of[c][target].astype(jnp.float32)).astype(jnp.bfloat16)

            @pl.when(exists & jnp.logical_not(behind))
            def _():
                held[k] = term_of[c][target]

            @pl.when(exists)
            def _():
                rs_copy(c, k, way).start()

    def gate_up(c, first, last):
        expert, size = CHUNKS[c]
        m = n * size

        @pl.loop(first, last)
        def _(i):
            at = pl.ds(pl.multiple_of(i * f_tile, f_tile), f_tile)
            x = rows_of[c][...].reshape(m, features)
            dims = (((1,), (1,)), ((), ()))
            g = lax.dot_general(x, gate[expert, at, :], dims, preferred_element_type=jnp.float32)
            u = lax.dot_general(x, up[expert, at, :], dims, preferred_element_type=jnp.float32)
            hidden[0:m, at] = (g / (1.0 + jnp.exp(-g)) * u).astype(jnp.bfloat16)

    def project(c, first, last):
        expert, size = CHUNKS[c]
        m = n * size

        @pl.loop(first, last)
        def _(j):
            at = pl.ds(pl.multiple_of(j * D_TILE, D_TILE), D_TILE)
            y = jnp.dot(hidden[0:m, :], down[expert, :, at], preferred_element_type=jnp.float32)
            term_of[c][:, :, at] = y.astype(jnp.bfloat16).reshape(n, size, D_TILE)

    events = sorted(((n - 1) * u + (k if k > 0 else -1), u, k) for u in range(len(units_of)) for k in range(n))
    ready = [max(i for i, (_, u, _) in enumerate(events) if units_of[u][0] == c) + 1 for c in range(count)]
    for _, u, k in events[: ready[0]]:
        gather(u, k)

    for c, (expert, size) in enumerate(CHUNKS):
        first_use = c == 0 or CHUNKS[c - 1][0] != expert
        pieces = [functools.partial(gate_up, c, i, i + 1) for i in range(f_steps)]
        pieces += [functools.partial(project, c, i, i + 1) for i in range(d_steps)]
        services = []
        if c + 1 < count:
            own_events = events[ready[c] : ready[c + 1]]
            services += [((i + 1) / (len(own_events) + 1), 1, i, functools.partial(gather, u, k)) for i, (_, u, k) in enumerate(own_events)]
        if c > 0:
            services += [(i / (n - 1), 0, i, functools.partial(rs_step, c - 1, n - 1 - i)) for i in range(1, n - 1)]
        services.sort(key=lambda entry: entry[:3])
        if first_use:
            load(0, expert).wait()
            load(1, expert).wait()
        if c == 0:
            for index in range(3):
                load(index, 1).start()
        done = 0
        for i, piece in enumerate(pieces):
            if first_use and i == f_steps:
                load(2, expert).wait()
            piece()
            while done < len(services) and services[done][0] * len(pieces) <= i + 1:
                services[done][3]()
                done += 1
        rs_step(c, n - 1)
        for entry in services[done:]:
            entry[3]()
    for k in range(n - 2, 0, -1):
        rs_step(count - 1, k)

    for c, (_, size) in enumerate(CHUNKS):
        at = pl.ds(starts[c], size)
        own[at, :] = term_of[c][p]

        @pl.when(has_left)
        def _():
            rs_wait(c, 0, 0)

        @pl.when(has_right)
        def _():
            rs_wait(c, 0, 1)

        @pl.when(has_left & has_right)
        def _():
            total = right_of[c][0].astype(jnp.float32) + left_of[c][0].astype(jnp.float32)
            own[at, :] = (total + term_of[c][p].astype(jnp.float32)).astype(jnp.bfloat16)

        @pl.when(has_left & jnp.logical_not(has_right))
        def _():
            own[at, :] = (right_of[c][0].astype(jnp.float32) + term_of[c][p].astype(jnp.float32)).astype(jnp.bfloat16)

        @pl.when(has_right & jnp.logical_not(has_left))
        def _():
            own[at, :] = (left_of[c][0].astype(jnp.float32) + term_of[c][p].astype(jnp.float32)).astype(jnp.bfloat16)

    for u in range(len(units_of)):
        for k in range(n - 1):
            ag_each(u, k, lambda copy: copy.wait_send())
    for c in range(count):
        for k in range(1, n):

            @pl.when(p + k <= n - 1)
            def _():
                rs_copy(c, k, 0).wait_send()

            @pl.when(p - k >= 0)
            def _():
                rs_copy(c, k, 1).wait_send()


def body(n, tokens, expert_ids, route_logits, w_gate, w_up, w_down):
    count, features, units = len(CHUNKS), tokens.shape[1], w_gate.shape[1]
    unit_count = sum(size // UNIT for _, size in CHUNKS)
    most = max(size for _, size in CHUNKS)
    per_chunk = [pltpu.VMEM((n, size, features), jnp.bfloat16) for _, size in CHUNKS]
    vmem = pl.BlockSpec(memory_space=pltpu.VMEM)
    hbm = pl.BlockSpec(memory_space=pl.ANY)
    weights = pltpu.VMEM((EXP_WIN, units, features), jnp.bfloat16)
    own, weighted = pl.pallas_call(
        functools.partial(kernel, n),
        out_shape=(
            jax.ShapeDtypeStruct((EXP_WIN * CAP, features), jnp.bfloat16),
            jax.ShapeDtypeStruct((EXP_WIN * CAP, tokens.shape[0]), jnp.bfloat16),
        ),
        in_specs=[vmem, vmem, vmem, hbm, hbm, hbm],
        out_specs=(vmem, vmem),
        scratch_shapes=per_chunk * 4
        + [
            weights,
            weights,
            weights,
            pltpu.VMEM((n * most, units), jnp.bfloat16),
            pltpu.SemaphoreType.DMA((3, EXP_WIN)),
            pltpu.SemaphoreType.DMA((2, unit_count, n)),
            pltpu.SemaphoreType.DMA((2, unit_count, n)),
            pltpu.SemaphoreType.DMA((2, count, n)),
            pltpu.SemaphoreType.DMA((2, count, n)),
        ],
        compiler_params=pltpu.CompilerParams(collective_id=0, has_side_effects=True, vmem_limit_bytes=60 * 2**20),
    )(tokens, expert_ids.T, route_logits.T, w_gate, w_up, w_down)
    mixed = lax.dot_general(weighted, own, (((0,), (0,)), ((), ())), preferred_element_type=jnp.float32)
    return mixed.astype(jnp.bfloat16)


def solution(mesh):
    in_specs = (
        P(("rep", "et"), None),
        P(("rep", "et"), None),
        P(("rep", "et"), None),
        P(None, "et", None),
        P(None, "et", None),
        P(None, "et", None),
    )
    out_specs = P(("rep", "et"), None)
    return jax.shard_map(
        functools.partial(body, mesh.shape["et"]), mesh=mesh, in_specs=in_specs, out_specs=out_specs, check_vma=False
    )
```

```python
import functools

import jax
import jax.numpy as jnp
from jax import lax
from jax.experimental import pallas as pl
from jax.experimental.pallas import tpu as pltpu
from jax.sharding import PartitionSpec as P

EXP_WIN = 2
CAP = 48
ROWS = 48
UNIT = 16
F_TILE = 256
D_TILE = 512
AG_INSIDE = 5
MESH = pl.DeviceIdType.MESH


def routing(ids, logits):
    rows, slots = ids.shape[1], EXP_WIN * CAP
    low, high = logits[0:1, :], logits[1:2, :]
    top = jnp.maximum(low, high)
    exp_low, exp_high = jnp.exp(low - top), jnp.exp(high - top)
    total = exp_low + exp_high
    prob_low = (exp_low / total).astype(jnp.bfloat16).astype(jnp.float32)
    prob_high = (exp_high / total).astype(jnp.bfloat16).astype(jnp.float32)
    slot = lax.broadcasted_iota(jnp.int32, (slots, rows), 0)
    expert = jnp.where(slot >= CAP, 1, 0)
    in_low, in_high = ids[0:1, :] == expert, ids[1:2, :] == expert
    weight = jnp.where(in_low, prob_low, 0.0) + jnp.where(in_high, prob_high, 0.0)
    routed = jnp.where(in_low, 1.0, 0.0) + jnp.where(in_high, 1.0, 0.0)
    upper = lax.broadcasted_iota(jnp.int32, (rows, rows), 0) <= lax.broadcasted_iota(jnp.int32, (rows, rows), 1)
    ranking = jnp.dot(
        routed.astype(jnp.bfloat16), jnp.where(upper, 1.0, 0.0).astype(jnp.bfloat16), preferred_element_type=jnp.float32
    )
    place = (slot - CAP * expert + 1).astype(jnp.float32)
    selected = jnp.where(ranking == place, routed, 0.0)
    return selected.astype(jnp.bfloat16), (selected * weight).astype(jnp.bfloat16)


def kernel(n, tokens, ids, logits, w_gate, w_up, w_down, own, weighted, *scratch):
    rows, terms, right, left, gate, up, down, hidden, total, load_sem, ag_send, ag_recv, rs_send, rs_recv = scratch
    p = lax.axis_index("et")
    features, units = tokens.shape[1], gate.shape[1]
    count, parts = EXP_WIN * CAP // ROWS, ROWS // UNIT
    per_expert = CAP // ROWS
    m = n * ROWS
    f_tile = F_TILE if units % F_TILE == 0 else units
    f_steps, d_steps = units // f_tile, features // D_TILE
    steps = f_steps + d_steps
    has_left, has_right = p > 0, p < n - 1

    def load(index, expert):
        source, held = ((w_gate, gate), (w_up, up), (w_down, down))[index]
        return pltpu.make_async_copy(source.at[expert], held.at[expert], load_sem.at[index, expert])

    for index in range(3):
        load(index, 0).start()

    barrier = pltpu.get_barrier_semaphore()

    @pl.when(has_left)
    def _():
        pl.semaphore_signal(barrier, inc=1, device_id={"et": p - 1}, device_id_type=MESH)

    @pl.when(has_right)
    def _():
        pl.semaphore_signal(barrier, inc=1, device_id={"et": p + 1}, device_id_type=MESH)

    plain, scaled = routing(ids[...], logits[...])
    weighted[...] = scaled
    for part in range(d_steps):
        columns = pl.ds(part * D_TILE, D_TILE)
        picked = jnp.dot(plain, tokens[:, columns], preferred_element_type=jnp.float32).astype(jnp.bfloat16)
        for c in range(count):
            rows[c, p, :, columns] = picked[c * ROWS : (c + 1) * ROWS]

    pl.semaphore_wait(barrier, jnp.where(has_left & has_right, 2, 1))

    def span(u):
        return pl.ds(pl.multiple_of(u * UNIT, UNIT), UNIT)

    def ag_copy(c, u, k, way, arriving=False):
        source = p - k if way == 0 else p + k
        held = rows.at[c, source, span(u)]
        step = k - 1 if arriving else k
        return pltpu.make_async_remote_copy(
            src_ref=held,
            dst_ref=held,
            send_sem=ag_send.at[way, c, u, step],
            recv_sem=ag_recv.at[way, c, u, step + 1],
            device_id={"et": p + 1 if (way == 0) != arriving else p - 1},
            device_id_type=MESH,
        )

    def ag_each(c, u, k, act):
        @pl.when((p - k >= 0) & has_right & (k < n - 1))
        def _():
            act(ag_copy(c, u, k, 0))

        @pl.when((p + k <= n - 1) & has_left & (k < n - 1))
        def _():
            act(ag_copy(c, u, k, 1))

    def ag_event(c, event):
        k, u = 1 + event // parts, event % parts

        @pl.when(p - k >= 0)
        def _():
            ag_copy(c, u, k, 0, True).wait_recv()

        @pl.when(p + k <= n - 1)
        def _():
            ag_copy(c, u, k, 1, True).wait_recv()

        ag_each(c, u, k, lambda copy: copy.start())

        @pl.when((k == n - 1) & (c + 1 < count))
        def _():
            ag_each(c + 1, u, 0, lambda copy: copy.start())

    def rs_copy(c, u, k, way, arriving=False):
        held = (right, left)[way]
        step = k + 1 if arriving else k
        return pltpu.make_async_remote_copy(
            src_ref=held.at[c, step, span(u)],
            dst_ref=held.at[c, step - 1, span(u)],
            send_sem=rs_send.at[way, c, u, step],
            recv_sem=rs_recv.at[way, c, u, step - 1],
            device_id={"et": p + 1 if (way == 0) != arriving else p - 1},
            device_id_type=MESH,
        )

    def rs_event(c, event):
        k, u = n - 1 - event // parts, event % parts
        for way in range(2):
            held = (right, left)[way]
            target = p + k if way == 0 else p - k
            exists = target <= n - 1 if way == 0 else target >= 0
            behind = has_left if way == 0 else has_right

            @pl.when(exists & behind)
            def _():
                rs_copy(c, u, k, way, True).wait_recv()
                summed = held[c, k, span(u)].astype(jnp.float32) + terms[c, target, span(u)].astype(jnp.float32)
                held[c, k, span(u)] = summed.astype(jnp.bfloat16)

            @pl.when(exists & jnp.logical_not(behind))
            def _():
                held[c, k, span(u)] = terms[c, target, span(u)]

            @pl.when(exists)
            def _():
                rs_copy(c, u, k, way).start()

    ag_events = (n - 1) * parts
    ag_inside = min(ag_events, AG_INSIDE * ag_events // 9)
    rs_events = (n - 2) * parts

    @pl.loop(0, parts)
    def _(u):
        ag_each(0, u, 0, lambda copy: copy.start())

    @pl.loop(0, ag_events)
    def _(event):
        ag_event(0, event)

    @pl.loop(0, count)
    def _(c):
        expert = c // per_expert
        first_use = c % per_expert == 0

        @pl.loop(0, steps)
        def _(i):
            @pl.when((i == 0) & first_use)
            def _():
                load(0, expert).wait()
                load(1, expert).wait()

            @pl.when((i == 0) & (c == 0))
            def _():
                for index in range(3):
                    load(index, 1).start()

            @pl.when((i == f_steps) & first_use)
            def _():
                load(2, expert).wait()

            @pl.when(i < f_steps)
            def _():
                at = pl.ds(pl.multiple_of(i * f_tile, f_tile) if f_steps > 1 else 0, f_tile)
                x = rows[c].reshape(m, features)
                dims = (((1,), (1,)), ((), ()))
                g = lax.dot_general(x, gate[expert, at, :], dims, preferred_element_type=jnp.float32)
                u = lax.dot_general(x, up[expert, at, :], dims, preferred_element_type=jnp.float32)
                hidden[:, at] = (g / (1.0 + jnp.exp(-g)) * u).astype(jnp.bfloat16)

            @pl.when(i >= f_steps)
            def _():
                at = pl.ds(pl.multiple_of((i - f_steps) * D_TILE, D_TILE), D_TILE)
                y = jnp.dot(hidden[...], down[expert, :, at], preferred_element_type=jnp.float32)
                terms[c, :, :, at] = y.astype(jnp.bfloat16).reshape(n, ROWS, D_TILE)

            @pl.when(c > 0)
            def _():
                @pl.loop(i * rs_events // steps, (i + 1) * rs_events // steps)
                def _(event):
                    rs_event(c - 1, parts + event)

            @pl.when(c + 1 < count)
            def _():
                @pl.loop(i * ag_inside // steps, (i + 1) * ag_inside // steps)
                def _(event):
                    ag_event(c + 1, event)

        @pl.loop(0, parts)
        def _(event):
            rs_event(c, event)

        @pl.when(c + 1 < count)
        def _():
            @pl.loop(ag_inside, ag_events)
            def _(event):
                ag_event(c + 1, event)

    @pl.loop(parts, parts + rs_events)
    def _(event):
        rs_event(count - 1, event)

    @pl.loop(0, count * parts)
    def _(unit):
        c, u = unit // parts, unit % parts
        total[...] = terms[c, p, span(u)].astype(jnp.float32)

        @pl.when(has_left)
        def _():
            rs_copy(c, u, 0, 0, True).wait_recv()
            total[...] += right[c, 0, span(u)].astype(jnp.float32)

        @pl.when(has_right)
        def _():
            rs_copy(c, u, 0, 1, True).wait_recv()
            total[...] += left[c, 0, span(u)].astype(jnp.float32)

        own[span(unit), :] = total[...].astype(jnp.bfloat16)

    @pl.loop(0, count * parts)
    def _(unit):
        c, u = unit // parts, unit % parts

        @pl.loop(0, n - 1)
        def _(k):
            ag_each(c, u, k, lambda copy: copy.wait_send())

            @pl.when(p + k + 1 <= n - 1)
            def _():
                rs_copy(c, u, k + 1, 0).wait_send()

            @pl.when(p - k - 1 >= 0)
            def _():
                rs_copy(c, u, k + 1, 1).wait_send()


def body(n, tokens, expert_ids, route_logits, w_gate, w_up, w_down):
    count, features, units = EXP_WIN * CAP // ROWS, tokens.shape[1], w_gate.shape[1]
    blocks = pltpu.VMEM((count, n, ROWS, features), jnp.bfloat16)
    semaphores = pltpu.SemaphoreType.DMA((2, count, ROWS // UNIT, n))
    vmem = pl.BlockSpec(memory_space=pltpu.VMEM)
    hbm = pl.BlockSpec(memory_space=pl.ANY)
    weights = pltpu.VMEM((EXP_WIN, units, features), jnp.bfloat16)
    own, weighted = pl.pallas_call(
        functools.partial(kernel, n),
        out_shape=(
            jax.ShapeDtypeStruct((EXP_WIN * CAP, features), jnp.bfloat16),
            jax.ShapeDtypeStruct((EXP_WIN * CAP, tokens.shape[0]), jnp.bfloat16),
        ),
        in_specs=[vmem, vmem, vmem, hbm, hbm, hbm],
        out_specs=(vmem, vmem),
        scratch_shapes=[
            blocks,
            blocks,
            blocks,
            blocks,
            weights,
            weights,
            weights,
            pltpu.VMEM((n * ROWS, units), jnp.bfloat16),
            pltpu.VMEM((UNIT, features), jnp.float32),
            pltpu.SemaphoreType.DMA((3, EXP_WIN)),
            semaphores,
            semaphores,
            semaphores,
            semaphores,
        ],
        compiler_params=pltpu.CompilerParams(collective_id=0, has_side_effects=True, vmem_limit_bytes=60 * 2**20),
    )(tokens, expert_ids.T, route_logits.T, w_gate, w_up, w_down)
    mixed = lax.dot_general(weighted, own, (((0,), (0,)), ((), ())), preferred_element_type=jnp.float32)
    return mixed.astype(jnp.bfloat16)


def solution(mesh):
    in_specs = (
        P(("rep", "et"), None),
        P(("rep", "et"), None),
        P(("rep", "et"), None),
        P(None, "et", None),
        P(None, "et", None),
        P(None, "et", None),
    )
    out_specs = P(("rep", "et"), None)
    return jax.shard_map(
        functools.partial(body, mesh.shape["et"]), mesh=mesh, in_specs=in_specs, out_specs=out_specs, check_vma=False
    )
```

```python
import functools

import jax
import jax.numpy as jnp
from jax import lax
from jax.experimental import pallas as pl
from jax.experimental.pallas import tpu as pltpu
from jax.sharding import PartitionSpec as P

EXP_WIN = 2
CAP = 48
ROWS = 48
UNIT = 16
F_TILE = 896
D_TILE = 512
AG_INSIDE = 5
MESH = pl.DeviceIdType.MESH


def routing(ids, logits):
    rows, slots = ids.shape[1], EXP_WIN * CAP
    low, high = logits[0:1, :], logits[1:2, :]
    top = jnp.maximum(low, high)
    exp_low, exp_high = jnp.exp(low - top), jnp.exp(high - top)
    total = exp_low + exp_high
    prob_low = (exp_low / total).astype(jnp.bfloat16).astype(jnp.float32)
    prob_high = (exp_high / total).astype(jnp.bfloat16).astype(jnp.float32)
    slot = lax.broadcasted_iota(jnp.int32, (slots, rows), 0)
    expert = jnp.where(slot >= CAP, 1, 0)
    in_low, in_high = ids[0:1, :] == expert, ids[1:2, :] == expert
    weight = jnp.where(in_low, prob_low, 0.0) + jnp.where(in_high, prob_high, 0.0)
    routed = jnp.where(in_low, 1.0, 0.0) + jnp.where(in_high, 1.0, 0.0)
    upper = lax.broadcasted_iota(jnp.int32, (rows, rows), 0) <= lax.broadcasted_iota(jnp.int32, (rows, rows), 1)
    ranking = jnp.dot(
        routed.astype(jnp.bfloat16), jnp.where(upper, 1.0, 0.0).astype(jnp.bfloat16), preferred_element_type=jnp.float32
    )
    place = (slot - CAP * expert + 1).astype(jnp.float32)
    selected = jnp.where(ranking == place, routed, 0.0)
    return selected.astype(jnp.bfloat16), (selected * weight).astype(jnp.bfloat16)


def kernel(n, tokens, ids, logits, w_gate, w_up, w_down, own, weighted, *scratch):
    rows, terms, right, left, gate, up, down, turned, hidden, total, load_sem, ag_send, ag_recv, rs_send, rs_recv = scratch
    p = lax.axis_index("et")
    features, units = tokens.shape[1], gate.shape[1]
    count, parts = EXP_WIN * CAP // ROWS, ROWS // UNIT
    per_expert = CAP // ROWS
    m = n * ROWS
    f_tile = F_TILE if units % F_TILE == 0 else units
    f_steps, d_steps = units // f_tile, features // D_TILE
    steps = f_steps + d_steps
    has_left, has_right = p > 0, p < n - 1

    def load(index, expert):
        source, held = ((w_gate, gate), (w_up, up), (w_down, down))[index]
        return pltpu.make_async_copy(source.at[expert], held.at[expert], load_sem.at[index, expert])

    for index in range(3):
        load(index, 0).start()

    barrier = pltpu.get_barrier_semaphore()

    @pl.when(has_left)
    def _():
        pl.semaphore_signal(barrier, inc=1, device_id={"et": p - 1}, device_id_type=MESH)

    @pl.when(has_right)
    def _():
        pl.semaphore_signal(barrier, inc=1, device_id={"et": p + 1}, device_id_type=MESH)

    plain, scaled = routing(ids[...], logits[...])
    weighted[...] = scaled
    for part in range(d_steps):
        columns = pl.ds(part * D_TILE, D_TILE)
        picked = jnp.dot(plain, tokens[:, columns], preferred_element_type=jnp.float32).astype(jnp.bfloat16)
        for c in range(count):
            rows[c, p, :, columns] = picked[c * ROWS : (c + 1) * ROWS]

    pl.semaphore_wait(barrier, jnp.where(has_left & has_right, 2, 1))

    def span(u):
        return pl.ds(pl.multiple_of(u * UNIT, UNIT), UNIT)

    def ag_copy(c, u, k, way, arriving=False):
        source = p - k if way == 0 else p + k
        held = rows.at[c, source, span(u)]
        step = k - 1 if arriving else k
        return pltpu.make_async_remote_copy(
            src_ref=held,
            dst_ref=held,
            send_sem=ag_send.at[way, c, u, step],
            recv_sem=ag_recv.at[way, c, u, step + 1],
            device_id={"et": p + 1 if (way == 0) != arriving else p - 1},
            device_id_type=MESH,
        )

    def ag_each(c, u, k, act):
        @pl.when((p - k >= 0) & has_right & (k < n - 1))
        def _():
            act(ag_copy(c, u, k, 0))

        @pl.when((p + k <= n - 1) & has_left & (k < n - 1))
        def _():
            act(ag_copy(c, u, k, 1))

    def ag_event(c, event):
        k, u = 1 + event // parts, event % parts

        @pl.when(p - k >= 0)
        def _():
            ag_copy(c, u, k, 0, True).wait_recv()

        @pl.when(p + k <= n - 1)
        def _():
            ag_copy(c, u, k, 1, True).wait_recv()

        ag_each(c, u, k, lambda copy: copy.start())

        @pl.when((k == n - 1) & (c + 1 < count))
        def _():
            ag_each(c + 1, u, 0, lambda copy: copy.start())

    def rs_copy(c, u, k, way, arriving=False):
        held = (right, left)[way]
        step = k + 1 if arriving else k
        return pltpu.make_async_remote_copy(
            src_ref=held.at[c, step, span(u)],
            dst_ref=held.at[c, step - 1, span(u)],
            send_sem=rs_send.at[way, c, u, step],
            recv_sem=rs_recv.at[way, c, u, step - 1],
            device_id={"et": p + 1 if (way == 0) != arriving else p - 1},
            device_id_type=MESH,
        )

    def rs_event(c, event):
        k, u = n - 1 - event // parts, event % parts
        for way in range(2):
            held = (right, left)[way]
            target = p + k if way == 0 else p - k
            exists = target <= n - 1 if way == 0 else target >= 0
            behind = has_left if way == 0 else has_right

            @pl.when(exists & behind)
            def _():
                rs_copy(c, u, k, way, True).wait_recv()
                summed = held[c, k, span(u)].astype(jnp.float32) + terms[c, target, span(u)].astype(jnp.float32)
                held[c, k, span(u)] = summed.astype(jnp.bfloat16)

            @pl.when(exists & jnp.logical_not(behind))
            def _():
                held[c, k, span(u)] = terms[c, target, span(u)]

            @pl.when(exists)
            def _():
                rs_copy(c, u, k, way).start()

    ag_events = (n - 1) * parts
    ag_inside = min(ag_events, AG_INSIDE * ag_events // 9)
    rs_events = (n - 2) * parts

    @pl.loop(0, parts)
    def _(u):
        ag_each(0, u, 0, lambda copy: copy.start())

    @pl.loop(0, ag_events)
    def _(event):
        ag_event(0, event)

    @pl.loop(0, count)
    def _(c):
        expert = c // per_expert
        first_use = c % per_expert == 0

        @pl.loop(0, d_steps)
        def _(j):
            at = pl.ds(pl.multiple_of(j * D_TILE, D_TILE), D_TILE)
            turned[at, :] = rows[c, :, :, at].reshape(m, D_TILE).T

        @pl.loop(0, steps)
        def _(i):
            @pl.when((i == 0) & first_use)
            def _():
                load(0, expert).wait()
                load(1, expert).wait()

            @pl.when((i == 0) & (c == 0))
            def _():
                for index in range(3):
                    load(index, 1).start()

            @pl.when((i == f_steps) & first_use)
            def _():
                load(2, expert).wait()

            @pl.when(i < f_steps)
            def _():
                at = pl.ds(pl.multiple_of(i * f_tile, f_tile) if f_steps > 1 else 0, f_tile)
                g = jnp.dot(gate[expert, at, :], turned[...], preferred_element_type=jnp.float32)
                u = jnp.dot(up[expert, at, :], turned[...], preferred_element_type=jnp.float32)
                hidden[:, at] = (g / (1.0 + jnp.exp(-g)) * u).astype(jnp.bfloat16).T

            @pl.when(i >= f_steps)
            def _():
                at = pl.ds(pl.multiple_of((i - f_steps) * D_TILE, D_TILE), D_TILE)
                y = jnp.dot(hidden[...], down[expert, :, at], preferred_element_type=jnp.float32)
                terms[c, :, :, at] = y.astype(jnp.bfloat16).reshape(n, ROWS, D_TILE)

            @pl.when(c > 0)
            def _():
                @pl.loop(i * rs_events // steps, (i + 1) * rs_events // steps)
                def _(event):
                    rs_event(c - 1, parts + event)

            @pl.when(c + 1 < count)
            def _():
                @pl.loop(i * ag_inside // steps, (i + 1) * ag_inside // steps)
                def _(event):
                    ag_event(c + 1, event)

        @pl.loop(0, parts)
        def _(event):
            rs_event(c, event)

        @pl.when(c + 1 < count)
        def _():
            @pl.loop(ag_inside, ag_events)
            def _(event):
                ag_event(c + 1, event)

    @pl.loop(parts, parts + rs_events)
    def _(event):
        rs_event(count - 1, event)

    @pl.loop(0, count * parts)
    def _(unit):
        c, u = unit // parts, unit % parts
        total[...] = terms[c, p, span(u)].astype(jnp.float32)

        @pl.when(has_left)
        def _():
            rs_copy(c, u, 0, 0, True).wait_recv()
            total[...] += right[c, 0, span(u)].astype(jnp.float32)

        @pl.when(has_right)
        def _():
            rs_copy(c, u, 0, 1, True).wait_recv()
            total[...] += left[c, 0, span(u)].astype(jnp.float32)

        own[span(unit), :] = total[...].astype(jnp.bfloat16)

    @pl.loop(0, count * parts)
    def _(unit):
        c, u = unit // parts, unit % parts

        @pl.loop(0, n - 1)
        def _(k):
            ag_each(c, u, k, lambda copy: copy.wait_send())

            @pl.when(p + k + 1 <= n - 1)
            def _():
                rs_copy(c, u, k + 1, 0).wait_send()

            @pl.when(p - k - 1 >= 0)
            def _():
                rs_copy(c, u, k + 1, 1).wait_send()


def body(n, tokens, expert_ids, route_logits, w_gate, w_up, w_down):
    count, features, units = EXP_WIN * CAP // ROWS, tokens.shape[1], w_gate.shape[1]
    blocks = pltpu.VMEM((count, n, ROWS, features), jnp.bfloat16)
    semaphores = pltpu.SemaphoreType.DMA((2, count, ROWS // UNIT, n))
    vmem = pl.BlockSpec(memory_space=pltpu.VMEM)
    hbm = pl.BlockSpec(memory_space=pl.ANY)
    weights = pltpu.VMEM((EXP_WIN, units, features), jnp.bfloat16)
    own, weighted = pl.pallas_call(
        functools.partial(kernel, n),
        out_shape=(
            jax.ShapeDtypeStruct((EXP_WIN * CAP, features), jnp.bfloat16),
            jax.ShapeDtypeStruct((EXP_WIN * CAP, tokens.shape[0]), jnp.bfloat16),
        ),
        in_specs=[vmem, vmem, vmem, hbm, hbm, hbm],
        out_specs=(vmem, vmem),
        scratch_shapes=[
            blocks,
            blocks,
            blocks,
            blocks,
            weights,
            weights,
            weights,
            pltpu.VMEM((features, n * ROWS), jnp.bfloat16),
            pltpu.VMEM((n * ROWS, units), jnp.bfloat16),
            pltpu.VMEM((UNIT, features), jnp.float32),
            pltpu.SemaphoreType.DMA((3, EXP_WIN)),
            semaphores,
            semaphores,
            semaphores,
            semaphores,
        ],
        compiler_params=pltpu.CompilerParams(collective_id=0, has_side_effects=True, vmem_limit_bytes=60 * 2**20),
    )(tokens, expert_ids.T, route_logits.T, w_gate, w_up, w_down)
    mixed = lax.dot_general(weighted, own, (((0,), (0,)), ((), ())), preferred_element_type=jnp.float32)
    return mixed.astype(jnp.bfloat16)


def solution(mesh):
    in_specs = (
        P(("rep", "et"), None),
        P(("rep", "et"), None),
        P(("rep", "et"), None),
        P(None, "et", None),
        P(None, "et", None),
        P(None, "et", None),
    )
    out_specs = P(("rep", "et"), None)
    return jax.shard_map(
        functools.partial(body, mesh.shape["et"]), mesh=mesh, in_specs=in_specs, out_specs=out_specs, check_vma=False
    )
```

```python
import functools

import jax
import jax.numpy as jnp
from jax import lax
from jax.experimental import pallas as pl
from jax.experimental.pallas import tpu as pltpu
from jax.sharding import PartitionSpec as P

EXP_WIN = 2
CAP = 48
ROWS = 16
UNIT = 16
F_TILE = 256
D_TILE = 512
AG_INSIDE = 6
MESH = pl.DeviceIdType.MESH


def routing(ids, logits):
    rows, slots = ids.shape[1], EXP_WIN * CAP
    low, high = logits[0:1, :], logits[1:2, :]
    top = jnp.maximum(low, high)
    exp_low, exp_high = jnp.exp(low - top), jnp.exp(high - top)
    total = exp_low + exp_high
    prob_low = (exp_low / total).astype(jnp.bfloat16).astype(jnp.float32)
    prob_high = (exp_high / total).astype(jnp.bfloat16).astype(jnp.float32)
    slot = lax.broadcasted_iota(jnp.int32, (slots, rows), 0)
    expert = jnp.where(slot >= CAP, 1, 0)
    in_low, in_high = ids[0:1, :] == expert, ids[1:2, :] == expert
    weight = jnp.where(in_low, prob_low, 0.0) + jnp.where(in_high, prob_high, 0.0)
    routed = jnp.where(in_low, 1.0, 0.0) + jnp.where(in_high, 1.0, 0.0)
    upper = lax.broadcasted_iota(jnp.int32, (rows, rows), 0) <= lax.broadcasted_iota(jnp.int32, (rows, rows), 1)
    ranking = jnp.dot(
        routed.astype(jnp.bfloat16), jnp.where(upper, 1.0, 0.0).astype(jnp.bfloat16), preferred_element_type=jnp.float32
    )
    place = (slot - CAP * expert + 1).astype(jnp.float32)
    selected = jnp.where(ranking == place, routed, 0.0)
    return selected.astype(jnp.bfloat16), (selected * weight).astype(jnp.bfloat16)


def kernel(n, tokens, ids, logits, w_gate, w_up, w_down, own, weighted, *scratch):
    rows, terms, right, left, gate, up, down, hidden, total, load_sem, ag_send, ag_recv, rs_send, rs_recv = scratch
    p = lax.axis_index("et")
    features, units = tokens.shape[1], gate.shape[1]
    count, parts = EXP_WIN * CAP // ROWS, ROWS // UNIT
    per_expert = CAP // ROWS
    m = n * ROWS
    f_tile = F_TILE if units % F_TILE == 0 else units
    f_steps, d_steps = units // f_tile, features // D_TILE
    steps = f_steps + d_steps
    has_left, has_right = p > 0, p < n - 1

    def load(index, expert):
        source, held = ((w_gate, gate), (w_up, up), (w_down, down))[index]
        return pltpu.make_async_copy(source.at[expert], held.at[expert], load_sem.at[index, expert])

    for index in range(3):
        load(index, 0).start()

    barrier = pltpu.get_barrier_semaphore()

    @pl.when(has_left)
    def _():
        pl.semaphore_signal(barrier, inc=1, device_id={"et": p - 1}, device_id_type=MESH)

    @pl.when(has_right)
    def _():
        pl.semaphore_signal(barrier, inc=1, device_id={"et": p + 1}, device_id_type=MESH)

    plain, scaled = routing(ids[...], logits[...])
    weighted[...] = scaled
    for part in range(d_steps):
        columns = pl.ds(part * D_TILE, D_TILE)
        picked = jnp.dot(plain, tokens[:, columns], preferred_element_type=jnp.float32).astype(jnp.bfloat16)
        for c in range(count):
            rows[c, p, :, columns] = picked[c * ROWS : (c + 1) * ROWS]

    pl.semaphore_wait(barrier, jnp.where(has_left & has_right, 2, 1))

    def span(u):
        return pl.ds(pl.multiple_of(u * UNIT, UNIT), UNIT)

    def ag_copy(c, u, k, way, arriving=False):
        source = p - k if way == 0 else p + k
        held = rows.at[c, source, span(u)]
        step = k - 1 if arriving else k
        return pltpu.make_async_remote_copy(
            src_ref=held,
            dst_ref=held,
            send_sem=ag_send.at[way, c, u, step],
            recv_sem=ag_recv.at[way, c, u, step + 1],
            device_id={"et": p + 1 if (way == 0) != arriving else p - 1},
            device_id_type=MESH,
        )

    def ag_each(c, u, k, act):
        @pl.when((p - k >= 0) & has_right & (k < n - 1))
        def _():
            act(ag_copy(c, u, k, 0))

        @pl.when((p + k <= n - 1) & has_left & (k < n - 1))
        def _():
            act(ag_copy(c, u, k, 1))

    def ag_event(c, event):
        k, u = 1 + event // parts, event % parts

        @pl.when(p - k >= 0)
        def _():
            ag_copy(c, u, k, 0, True).wait_recv()

        @pl.when(p + k <= n - 1)
        def _():
            ag_copy(c, u, k, 1, True).wait_recv()

        ag_each(c, u, k, lambda copy: copy.start())

        @pl.when((k == 1) & (c + 1 < count))
        def _():
            ag_each(c + 1, u, 0, lambda copy: copy.start())

    def rs_copy(c, u, k, way, arriving=False):
        held = (right, left)[way]
        step = k + 1 if arriving else k
        return pltpu.make_async_remote_copy(
            src_ref=held.at[c, step, span(u)],
            dst_ref=held.at[c, step - 1, span(u)],
            send_sem=rs_send.at[way, c, u, step],
            recv_sem=rs_recv.at[way, c, u, step - 1],
            device_id={"et": p + 1 if (way == 0) != arriving else p - 1},
            device_id_type=MESH,
        )

    def rs_event(c, event):
        k, u = n - 1 - event // parts, event % parts
        for way in range(2):
            held = (right, left)[way]
            target = p + k if way == 0 else p - k
            exists = target <= n - 1 if way == 0 else target >= 0
            behind = has_left if way == 0 else has_right

            @pl.when(exists & behind)
            def _():
                rs_copy(c, u, k, way, True).wait_recv()
                summed = held[c, k, span(u)].astype(jnp.float32) + terms[c, target, span(u)].astype(jnp.float32)
                held[c, k, span(u)] = summed.astype(jnp.bfloat16)

            @pl.when(exists & jnp.logical_not(behind))
            def _():
                held[c, k, span(u)] = terms[c, target, span(u)]

            @pl.when(exists)
            def _():
                rs_copy(c, u, k, way).start()

    ag_events = (n - 1) * parts
    ag_inside = min(ag_events, AG_INSIDE * ag_events // 9)
    rs_events = (n - 2) * parts

    @pl.loop(0, parts)
    def _(u):
        ag_each(0, u, 0, lambda copy: copy.start())

    for index in range(3):
        load(index, 1).start()

    @pl.loop(0, ag_events)
    def _(event):
        ag_event(0, event)

    @pl.loop(0, count)
    def _(c):
        expert = c // per_expert
        first_use = c % per_expert == 0

        @pl.loop(0, steps)
        def _(i):
            @pl.when((i == 0) & first_use)
            def _():
                load(0, expert).wait()
                load(1, expert).wait()

            @pl.when((i == f_steps) & first_use)
            def _():
                load(2, expert).wait()

            @pl.when(i < f_steps)
            def _():
                at = pl.ds(pl.multiple_of(i * f_tile, f_tile) if f_steps > 1 else 0, f_tile)
                x = rows[c].reshape(m, features)
                dims = (((1,), (1,)), ((), ()))
                g = lax.dot_general(x, gate[expert, at, :], dims, preferred_element_type=jnp.float32)
                u = lax.dot_general(x, up[expert, at, :], dims, preferred_element_type=jnp.float32)
                hidden[:, at] = (g / (1.0 + jnp.exp(-g)) * u).astype(jnp.bfloat16)

            @pl.when(i >= f_steps)
            def _():
                at = pl.ds(pl.multiple_of((i - f_steps) * D_TILE, D_TILE), D_TILE)
                y = jnp.dot(hidden[...], down[expert, :, at], preferred_element_type=jnp.float32)
                terms[c, :, :, at] = y.astype(jnp.bfloat16).reshape(n, ROWS, D_TILE)

            @pl.when(c > 0)
            def _():
                @pl.loop(i * rs_events // steps, (i + 1) * rs_events // steps)
                def _(event):
                    rs_event(c - 1, parts + event)

            @pl.when(c + 1 < count)
            def _():
                @pl.loop(i * ag_inside // steps, (i + 1) * ag_inside // steps)
                def _(event):
                    ag_event(c + 1, event)

        @pl.loop(0, parts)
        def _(event):
            rs_event(c, event)

        @pl.when(c + 1 < count)
        def _():
            @pl.loop(ag_inside, ag_events)
            def _(event):
                ag_event(c + 1, event)

    @pl.loop(parts, parts + rs_events)
    def _(event):
        rs_event(count - 1, event)

    @pl.loop(0, count * parts)
    def _(unit):
        c, u = unit // parts, unit % parts
        total[...] = terms[c, p, span(u)].astype(jnp.float32)

        @pl.when(has_left)
        def _():
            rs_copy(c, u, 0, 0, True).wait_recv()
            total[...] += right[c, 0, span(u)].astype(jnp.float32)

        @pl.when(has_right)
        def _():
            rs_copy(c, u, 0, 1, True).wait_recv()
            total[...] += left[c, 0, span(u)].astype(jnp.float32)

        own[span(unit), :] = total[...].astype(jnp.bfloat16)

    @pl.loop(0, count * parts)
    def _(unit):
        c, u = unit // parts, unit % parts

        @pl.loop(0, n - 1)
        def _(k):
            ag_each(c, u, k, lambda copy: copy.wait_send())

            @pl.when(p + k + 1 <= n - 1)
            def _():
                rs_copy(c, u, k + 1, 0).wait_send()

            @pl.when(p - k - 1 >= 0)
            def _():
                rs_copy(c, u, k + 1, 1).wait_send()


def body(n, tokens, expert_ids, route_logits, w_gate, w_up, w_down):
    count, features, units = EXP_WIN * CAP // ROWS, tokens.shape[1], w_gate.shape[1]
    blocks = pltpu.VMEM((count, n, ROWS, features), jnp.bfloat16)
    semaphores = pltpu.SemaphoreType.DMA((2, count, ROWS // UNIT, n))
    vmem = pl.BlockSpec(memory_space=pltpu.VMEM)
    hbm = pl.BlockSpec(memory_space=pl.ANY)
    weights = pltpu.VMEM((EXP_WIN, units, features), jnp.bfloat16)
    own, weighted = pl.pallas_call(
        functools.partial(kernel, n),
        out_shape=(
            jax.ShapeDtypeStruct((EXP_WIN * CAP, features), jnp.bfloat16),
            jax.ShapeDtypeStruct((EXP_WIN * CAP, tokens.shape[0]), jnp.bfloat16),
        ),
        in_specs=[vmem, vmem, vmem, hbm, hbm, hbm],
        out_specs=(vmem, vmem),
        scratch_shapes=[
            blocks,
            blocks,
            blocks,
            blocks,
            weights,
            weights,
            weights,
            pltpu.VMEM((n * ROWS, units), jnp.bfloat16),
            pltpu.VMEM((UNIT, features), jnp.float32),
            pltpu.SemaphoreType.DMA((3, EXP_WIN)),
            semaphores,
            semaphores,
            semaphores,
            semaphores,
        ],
        compiler_params=pltpu.CompilerParams(collective_id=0, has_side_effects=True, vmem_limit_bytes=60 * 2**20),
    )(tokens, expert_ids.T, route_logits.T, w_gate, w_up, w_down)
    mixed = lax.dot_general(weighted, own, (((0,), (0,)), ((), ())), preferred_element_type=jnp.float32)
    return mixed.astype(jnp.bfloat16)


def solution(mesh):
    in_specs = (
        P(("rep", "et"), None),
        P(("rep", "et"), None),
        P(("rep", "et"), None),
        P(None, "et", None),
        P(None, "et", None),
        P(None, "et", None),
    )
    out_specs = P(("rep", "et"), None)
    return jax.shard_map(
        functools.partial(body, mesh.shape["et"]), mesh=mesh, in_specs=in_specs, out_specs=out_specs, check_vma=False
    )
```

```python
import functools

import jax
import jax.numpy as jnp
from jax import lax
from jax.experimental import pallas as pl
from jax.experimental.pallas import tpu as pltpu
from jax.sharding import PartitionSpec as P

EXP_WIN = 2
CAP = 48
ROWS = 48
UNIT = 16
F_TILE = 256
D_TILE = 512
AG_INSIDE = 5
MESH = pl.DeviceIdType.MESH


def routing(ids, logits):
    rows, slots = ids.shape[1], EXP_WIN * CAP
    low, high = logits[0:1, :], logits[1:2, :]
    top = jnp.maximum(low, high)
    exp_low, exp_high = jnp.exp(low - top), jnp.exp(high - top)
    total = exp_low + exp_high
    prob_low = (exp_low / total).astype(jnp.bfloat16).astype(jnp.float32)
    prob_high = (exp_high / total).astype(jnp.bfloat16).astype(jnp.float32)
    slot = lax.broadcasted_iota(jnp.int32, (slots, rows), 0)
    expert = jnp.where(slot >= CAP, 1, 0)
    in_low, in_high = ids[0:1, :] == expert, ids[1:2, :] == expert
    weight = jnp.where(in_low, prob_low, 0.0) + jnp.where(in_high, prob_high, 0.0)
    routed = jnp.where(in_low, 1.0, 0.0) + jnp.where(in_high, 1.0, 0.0)
    upper = lax.broadcasted_iota(jnp.int32, (rows, rows), 0) <= lax.broadcasted_iota(jnp.int32, (rows, rows), 1)
    ranking = jnp.dot(
        routed.astype(jnp.bfloat16), jnp.where(upper, 1.0, 0.0).astype(jnp.bfloat16), preferred_element_type=jnp.float32
    )
    place = (slot - CAP * expert + 1).astype(jnp.float32)
    selected = jnp.where(ranking == place, routed, 0.0)
    return selected.astype(jnp.bfloat16), (selected * weight).astype(jnp.bfloat16)


def kernel(n, tokens, ids, logits, w_gate, w_up, w_down, own, weighted, *scratch):
    rows, terms, right, left, gate, up, down, hidden, total, load_sem, ag_send, ag_recv, rs_send, rs_recv = scratch
    p = lax.axis_index("et")
    features, units = tokens.shape[1], gate.shape[1]
    count, parts = EXP_WIN * CAP // ROWS, ROWS // UNIT
    per_expert = CAP // ROWS
    m = n * ROWS
    f_tile = F_TILE if units % F_TILE == 0 else units
    f_steps, d_steps = units // f_tile, features // D_TILE
    steps = f_steps + d_steps
    has_left, has_right = p > 0, p < n - 1

    def load(index, expert):
        source, held = ((w_gate, gate), (w_up, up), (w_down, down))[index]
        return pltpu.make_async_copy(source.at[expert], held.at[expert], load_sem.at[index, expert])

    for index in range(3):
        load(index, 0).start()

    barrier = pltpu.get_barrier_semaphore()

    @pl.when(has_left)
    def _():
        pl.semaphore_signal(barrier, inc=1, device_id={"et": p - 1}, device_id_type=MESH)

    @pl.when(has_right)
    def _():
        pl.semaphore_signal(barrier, inc=1, device_id={"et": p + 1}, device_id_type=MESH)

    plain, scaled = routing(ids[...], logits[...])
    weighted[...] = scaled
    for part in range(d_steps):
        columns = pl.ds(part * D_TILE, D_TILE)
        picked = jnp.dot(plain, tokens[:, columns], preferred_element_type=jnp.float32).astype(jnp.bfloat16)
        for c in range(count):
            rows[c, p, :, columns] = picked[c * ROWS : (c + 1) * ROWS]

    pl.semaphore_wait(barrier, jnp.where(has_left & has_right, 2, 1))

    def span(u):
        return pl.ds(pl.multiple_of(u * UNIT, UNIT), UNIT)

    def ag_copy(c, u, k, way, arriving=False):
        source = p - k if way == 0 else p + k
        held = rows.at[c, source, span(u)]
        step = k - 1 if arriving else k
        return pltpu.make_async_remote_copy(
            src_ref=held,
            dst_ref=held,
            send_sem=ag_send.at[way, c, u, step],
            recv_sem=ag_recv.at[way, c, u, step + 1],
            device_id={"et": p + 1 if (way == 0) != arriving else p - 1},
            device_id_type=MESH,
        )

    def ag_each(c, u, k, act):
        @pl.when((p - k >= 0) & has_right & (k < n - 1))
        def _():
            act(ag_copy(c, u, k, 0))

        @pl.when((p + k <= n - 1) & has_left & (k < n - 1))
        def _():
            act(ag_copy(c, u, k, 1))

    def ag_event(c, event):
        k, u = 1 + event // parts, event % parts

        @pl.when(p - k >= 0)
        def _():
            ag_copy(c, u, k, 0, True).wait_recv()

        @pl.when(p + k <= n - 1)
        def _():
            ag_copy(c, u, k, 1, True).wait_recv()

        ag_each(c, u, k, lambda copy: copy.start())

        @pl.when((k == n - 1) & (c + 1 < count))
        def _():
            ag_each(c + 1, u, 0, lambda copy: copy.start())

    def band(u):
        return pl.ds(pl.multiple_of(u * D_TILE, D_TILE), D_TILE)

    def rs_copy(c, u, k, way, arriving=False):
        held = (right, left)[way]
        step = k + 1 if arriving else k
        return pltpu.make_async_remote_copy(
            src_ref=held.at[c, step, :, band(u)],
            dst_ref=held.at[c, step - 1, :, band(u)],
            send_sem=rs_send.at[way, c, u, step],
            recv_sem=rs_recv.at[way, c, u, step - 1],
            device_id={"et": p + 1 if (way == 0) != arriving else p - 1},
            device_id_type=MESH,
        )

    def rs_event(c, event):
        k, u = n - 1 - event // d_steps, event % d_steps
        for way in range(2):
            held = (right, left)[way]
            target = p + k if way == 0 else p - k
            exists = target <= n - 1 if way == 0 else target >= 0
            behind = has_left if way == 0 else has_right

            @pl.when(exists & behind)
            def _():
                rs_copy(c, u, k, way, True).wait_recv()
                summed = held[c, k, :, band(u)].astype(jnp.float32) + terms[c, target, :, band(u)].astype(jnp.float32)
                held[c, k, :, band(u)] = summed.astype(jnp.bfloat16)

            @pl.when(exists & jnp.logical_not(behind))
            def _():
                held[c, k, :, band(u)] = terms[c, target, :, band(u)]

            @pl.when(exists)
            def _():
                rs_copy(c, u, k, way).start()

    ag_events = (n - 1) * parts
    ag_inside = min(ag_events, AG_INSIDE * ag_events // 9)
    rs_events = (n - 2) * d_steps

    @pl.loop(0, parts)
    def _(u):
        ag_each(0, u, 0, lambda copy: copy.start())

    for index in range(3):
        load(index, 1).start()

    @pl.loop(0, ag_events)
    def _(event):
        ag_event(0, event)

    @pl.loop(0, count)
    def _(c):
        expert = c // per_expert
        first_use = c % per_expert == 0

        @pl.loop(0, steps)
        def _(i):
            @pl.when((i == 0) & first_use)
            def _():
                load(0, expert).wait()
                load(1, expert).wait()

            @pl.when((i == f_steps) & first_use)
            def _():
                load(2, expert).wait()

            @pl.when(i < f_steps)
            def _():
                at = pl.ds(pl.multiple_of(i * f_tile, f_tile) if f_steps > 1 else 0, f_tile)
                x = rows[c].reshape(m, features)
                dims = (((1,), (1,)), ((), ()))
                g = lax.dot_general(x, gate[expert, at, :], dims, preferred_element_type=jnp.float32)
                u = lax.dot_general(x, up[expert, at, :], dims, preferred_element_type=jnp.float32)
                hidden[:, at] = (g / (1.0 + jnp.exp(-g)) * u).astype(jnp.bfloat16)

            @pl.when(i >= f_steps)
            def _():
                at = pl.ds(pl.multiple_of((i - f_steps) * D_TILE, D_TILE), D_TILE)
                y = jnp.dot(hidden[...], down[expert, :, at], preferred_element_type=jnp.float32)
                terms[c, :, :, at] = y.astype(jnp.bfloat16).reshape(n, ROWS, D_TILE)
                rs_event(c, i - f_steps)

            @pl.when(c > 0)
            def _():
                @pl.loop(i * rs_events // steps, (i + 1) * rs_events // steps)
                def _(event):
                    rs_event(c - 1, d_steps + event)

            @pl.when(c + 1 < count)
            def _():
                @pl.loop(i * ag_inside // steps, (i + 1) * ag_inside // steps)
                def _(event):
                    ag_event(c + 1, event)

        @pl.when(c + 1 < count)
        def _():
            @pl.loop(ag_inside, ag_events)
            def _(event):
                ag_event(c + 1, event)

    @pl.loop(d_steps, d_steps + rs_events)
    def _(event):
        rs_event(count - 1, event)

    @pl.loop(0, count * d_steps)
    def _(unit):
        c, u = unit // d_steps, unit % d_steps
        total[...] = terms[c, p, :, band(u)].astype(jnp.float32)

        @pl.when(has_left)
        def _():
            rs_copy(c, u, 0, 0, True).wait_recv()
            total[...] += right[c, 0, :, band(u)].astype(jnp.float32)

        @pl.when(has_right)
        def _():
            rs_copy(c, u, 0, 1, True).wait_recv()
            total[...] += left[c, 0, :, band(u)].astype(jnp.float32)

        own[pl.ds(pl.multiple_of(c * ROWS, ROWS), ROWS), band(u)] = total[...].astype(jnp.bfloat16)

    @pl.loop(0, n - 1)
    def _(k):
        @pl.loop(0, count * parts)
        def _(unit):
            ag_each(unit // parts, unit % parts, k, lambda copy: copy.wait_send())

        @pl.loop(0, count * d_steps)
        def _(unit):
            c, u = unit // d_steps, unit % d_steps

            @pl.when(p + k + 1 <= n - 1)
            def _():
                rs_copy(c, u, k + 1, 0).wait_send()

            @pl.when(p - k - 1 >= 0)
            def _():
                rs_copy(c, u, k + 1, 1).wait_send()


def body(n, tokens, expert_ids, route_logits, w_gate, w_up, w_down):
    count, features, units = EXP_WIN * CAP // ROWS, tokens.shape[1], w_gate.shape[1]
    blocks = pltpu.VMEM((count, n, ROWS, features), jnp.bfloat16)
    gather_semaphores = pltpu.SemaphoreType.DMA((2, count, ROWS // UNIT, n))
    sum_semaphores = pltpu.SemaphoreType.DMA((2, count, features // D_TILE, n))
    vmem = pl.BlockSpec(memory_space=pltpu.VMEM)
    hbm = pl.BlockSpec(memory_space=pl.ANY)
    weights = pltpu.VMEM((EXP_WIN, units, features), jnp.bfloat16)
    own, weighted = pl.pallas_call(
        functools.partial(kernel, n),
        out_shape=(
            jax.ShapeDtypeStruct((EXP_WIN * CAP, features), jnp.bfloat16),
            jax.ShapeDtypeStruct((EXP_WIN * CAP, tokens.shape[0]), jnp.bfloat16),
        ),
        in_specs=[vmem, vmem, vmem, hbm, hbm, hbm],
        out_specs=(vmem, vmem),
        scratch_shapes=[
            blocks,
            blocks,
            blocks,
            blocks,
            weights,
            weights,
            weights,
            pltpu.VMEM((n * ROWS, units), jnp.bfloat16),
            pltpu.VMEM((ROWS, D_TILE), jnp.float32),
            pltpu.SemaphoreType.DMA((3, EXP_WIN)),
            gather_semaphores,
            gather_semaphores,
            sum_semaphores,
            sum_semaphores,
        ],
        compiler_params=pltpu.CompilerParams(collective_id=0, has_side_effects=True, vmem_limit_bytes=60 * 2**20),
    )(tokens, expert_ids.T, route_logits.T, w_gate, w_up, w_down)
    mixed = lax.dot_general(weighted, own, (((0,), (0,)), ((), ())), preferred_element_type=jnp.float32)
    return mixed.astype(jnp.bfloat16)


def solution(mesh):
    in_specs = (
        P(("rep", "et"), None),
        P(("rep", "et"), None),
        P(("rep", "et"), None),
        P(None, "et", None),
        P(None, "et", None),
        P(None, "et", None),
    )
    out_specs = P(("rep", "et"), None)
    return jax.shard_map(
        functools.partial(body, mesh.shape["et"]), mesh=mesh, in_specs=in_specs, out_specs=out_specs, check_vma=False
    )
```

```python
import functools

import jax
import jax.numpy as jnp
from jax import lax
from jax.experimental import pallas as pl
from jax.experimental.pallas import tpu as pltpu
from jax.sharding import PartitionSpec as P

EXP_WIN = 2
CAP = 48
ROWS = 48
UNIT = 16
F_TILE = 256
D_TILE = 512
AG_INSIDE = 9
MESH = pl.DeviceIdType.MESH


def routing(ids, logits):
    rows, slots = ids.shape[1], EXP_WIN * CAP
    low, high = logits[0:1, :], logits[1:2, :]
    top = jnp.maximum(low, high)
    exp_low, exp_high = jnp.exp(low - top), jnp.exp(high - top)
    total = exp_low + exp_high
    prob_low = (exp_low / total).astype(jnp.bfloat16).astype(jnp.float32)
    prob_high = (exp_high / total).astype(jnp.bfloat16).astype(jnp.float32)
    slot = lax.broadcasted_iota(jnp.int32, (slots, rows), 0)
    expert = jnp.where(slot >= CAP, 1, 0)
    in_low, in_high = ids[0:1, :] == expert, ids[1:2, :] == expert
    weight = jnp.where(in_low, prob_low, 0.0) + jnp.where(in_high, prob_high, 0.0)
    routed = jnp.where(in_low, 1.0, 0.0) + jnp.where(in_high, 1.0, 0.0)
    upper = lax.broadcasted_iota(jnp.int32, (rows, rows), 0) <= lax.broadcasted_iota(jnp.int32, (rows, rows), 1)
    ranking = jnp.dot(
        routed.astype(jnp.bfloat16), jnp.where(upper, 1.0, 0.0).astype(jnp.bfloat16), preferred_element_type=jnp.float32
    )
    place = (slot - CAP * expert + 1).astype(jnp.float32)
    selected = jnp.where(ranking == place, routed, 0.0)
    return selected.astype(jnp.bfloat16), (selected * weight).astype(jnp.bfloat16)


def kernel(n, tokens, ids, logits, w_gate, w_up, w_down, own, weighted, *scratch):
    rows, terms, right, left, gate, up, down, hidden, total, load_sem, ag_send, ag_recv, rs_send, rs_recv = scratch
    p = lax.axis_index("et")
    features, units = tokens.shape[1], gate.shape[1]
    count, parts = EXP_WIN * CAP // ROWS, ROWS // UNIT
    per_expert = CAP // ROWS
    m = n * ROWS
    f_tile = F_TILE if units % F_TILE == 0 else units
    f_steps, d_steps = units // f_tile, features // D_TILE
    steps = f_steps + d_steps
    has_left, has_right = p > 0, p < n - 1

    def load(index, expert):
        source, held = ((w_gate, gate), (w_up, up), (w_down, down))[index]
        return pltpu.make_async_copy(source.at[expert], held.at[expert], load_sem.at[index, expert])

    for index in range(3):
        load(index, 0).start()

    barrier = pltpu.get_barrier_semaphore()

    @pl.when(has_left)
    def _():
        pl.semaphore_signal(barrier, inc=1, device_id={"et": p - 1}, device_id_type=MESH)

    @pl.when(has_right)
    def _():
        pl.semaphore_signal(barrier, inc=1, device_id={"et": p + 1}, device_id_type=MESH)

    plain, scaled = routing(ids[...], logits[...])
    weighted[...] = scaled
    for part in range(d_steps):
        columns = pl.ds(part * D_TILE, D_TILE)
        picked = jnp.dot(plain, tokens[:, columns], preferred_element_type=jnp.float32).astype(jnp.bfloat16)
        for c in range(count):
            rows[c, p, :, columns] = picked[c * ROWS : (c + 1) * ROWS]

    pl.semaphore_wait(barrier, jnp.where(has_left & has_right, 2, 1))

    def span(u):
        return pl.ds(pl.multiple_of(u * UNIT, UNIT), UNIT)

    def ag_copy(c, u, k, way, arriving=False):
        source = p - k if way == 0 else p + k
        held = rows.at[c, source, span(u)]
        step = k - 1 if arriving else k
        return pltpu.make_async_remote_copy(
            src_ref=held,
            dst_ref=held,
            send_sem=ag_send.at[way, c, u, step],
            recv_sem=ag_recv.at[way, c, u, step + 1],
            device_id={"et": p + 1 if (way == 0) != arriving else p - 1},
            device_id_type=MESH,
        )

    def ag_each(c, u, k, act):
        @pl.when((p - k >= 0) & has_right & (k < n - 1))
        def _():
            act(ag_copy(c, u, k, 0))

        @pl.when((p + k <= n - 1) & has_left & (k < n - 1))
        def _():
            act(ag_copy(c, u, k, 1))

    def ag_event(c, event):
        k, u = 1 + event // parts, event % parts

        @pl.when(p - k >= 0)
        def _():
            ag_copy(c, u, k, 0, True).wait_recv()

        @pl.when(p + k <= n - 1)
        def _():
            ag_copy(c, u, k, 1, True).wait_recv()

        ag_each(c, u, k, lambda copy: copy.start())

        @pl.when((k == max(n - 2, 1)) & (c + 1 < count))
        def _():
            ag_each(c + 1, u, 0, lambda copy: copy.start())

    def band(u):
        return pl.ds(pl.multiple_of(u * D_TILE, D_TILE), D_TILE)

    def rs_copy(c, u, k, way, arriving=False):
        held = (right, left)[way]
        step = k + 1 if arriving else k
        return pltpu.make_async_remote_copy(
            src_ref=held.at[c, step, :, band(u)],
            dst_ref=held.at[c, step - 1, :, band(u)],
            send_sem=rs_send.at[way, c, u, step],
            recv_sem=rs_recv.at[way, c, u, step - 1],
            device_id={"et": p + 1 if (way == 0) != arriving else p - 1},
            device_id_type=MESH,
        )

    def rs_event(c, event):
        k, u = n - 1 - event // d_steps, event % d_steps
        for way in range(2):
            held = (right, left)[way]
            target = p + k if way == 0 else p - k
            exists = target <= n - 1 if way == 0 else target >= 0
            behind = has_left if way == 0 else has_right

            @pl.when(exists & behind)
            def _():
                rs_copy(c, u, k, way, True).wait_recv()
                summed = held[c, k, :, band(u)].astype(jnp.float32) + terms[c, target, :, band(u)].astype(jnp.float32)
                held[c, k, :, band(u)] = summed.astype(jnp.bfloat16)

            @pl.when(exists & jnp.logical_not(behind))
            def _():
                held[c, k, :, band(u)] = terms[c, target, :, band(u)]

            @pl.when(exists)
            def _():
                rs_copy(c, u, k, way).start()

    ag_events = (n - 1) * parts
    ag_inside = min(ag_events, AG_INSIDE * ag_events // 9)
    rs_events = (n - 2) * d_steps

    @pl.loop(0, parts)
    def _(u):
        ag_each(0, u, 0, lambda copy: copy.start())

    for index in range(3):
        load(index, 1).start()

    @pl.loop(0, ag_events)
    def _(event):
        ag_event(0, event)

    @pl.loop(0, count)
    def _(c):
        expert = c // per_expert
        first_use = c % per_expert == 0

        @pl.loop(0, steps)
        def _(i):
            @pl.when((i == 0) & first_use)
            def _():
                load(0, expert).wait()
                load(1, expert).wait()

            @pl.when((i == f_steps) & first_use)
            def _():
                load(2, expert).wait()

            @pl.when(i < f_steps)
            def _():
                at = pl.ds(pl.multiple_of(i * f_tile, f_tile) if f_steps > 1 else 0, f_tile)
                x = rows[c].reshape(m, features)
                dims = (((1,), (1,)), ((), ()))
                g = lax.dot_general(x, gate[expert, at, :], dims, preferred_element_type=jnp.float32)
                u = lax.dot_general(x, up[expert, at, :], dims, preferred_element_type=jnp.float32)
                hidden[:, at] = (g / (1.0 + jnp.exp(-g)) * u).astype(jnp.bfloat16)

            @pl.when(i >= f_steps)
            def _():
                at = pl.ds(pl.multiple_of((i - f_steps) * D_TILE, D_TILE), D_TILE)
                y = jnp.dot(hidden[...], down[expert, :, at], preferred_element_type=jnp.float32)
                terms[c, :, :, at] = y.astype(jnp.bfloat16).reshape(n, ROWS, D_TILE)
                rs_event(c, i - f_steps)

            @pl.when(c > 0)
            def _():
                @pl.loop(i * rs_events // steps, (i + 1) * rs_events // steps)
                def _(event):
                    rs_event(c - 1, d_steps + event)

            @pl.when(c + 1 < count)
            def _():
                @pl.loop(i * ag_inside // steps, (i + 1) * ag_inside // steps)
                def _(event):
                    ag_event(c + 1, event)

        @pl.when(c + 1 < count)
        def _():
            @pl.loop(ag_inside, ag_events)
            def _(event):
                ag_event(c + 1, event)

    @pl.loop(d_steps, d_steps + rs_events)
    def _(event):
        rs_event(count - 1, event)

    @pl.loop(0, count * d_steps)
    def _(unit):
        c, u = unit // d_steps, unit % d_steps
        total[...] = terms[c, p, :, band(u)].astype(jnp.float32)

        @pl.when(has_left)
        def _():
            rs_copy(c, u, 0, 0, True).wait_recv()
            total[...] += right[c, 0, :, band(u)].astype(jnp.float32)

        @pl.when(has_right)
        def _():
            rs_copy(c, u, 0, 1, True).wait_recv()
            total[...] += left[c, 0, :, band(u)].astype(jnp.float32)

        own[pl.ds(pl.multiple_of(c * ROWS, ROWS), ROWS), band(u)] = total[...].astype(jnp.bfloat16)

    @pl.loop(0, n - 1)
    def _(k):
        @pl.loop(0, count * parts)
        def _(unit):
            ag_each(unit // parts, unit % parts, k, lambda copy: copy.wait_send())

        @pl.loop(0, count * d_steps)
        def _(unit):
            c, u = unit // d_steps, unit % d_steps

            @pl.when(p + k + 1 <= n - 1)
            def _():
                rs_copy(c, u, k + 1, 0).wait_send()

            @pl.when(p - k - 1 >= 0)
            def _():
                rs_copy(c, u, k + 1, 1).wait_send()


def body(n, tokens, expert_ids, route_logits, w_gate, w_up, w_down):
    count, features, units = EXP_WIN * CAP // ROWS, tokens.shape[1], w_gate.shape[1]
    blocks = pltpu.VMEM((count, n, ROWS, features), jnp.bfloat16)
    gather_semaphores = pltpu.SemaphoreType.DMA((2, count, ROWS // UNIT, n))
    sum_semaphores = pltpu.SemaphoreType.DMA((2, count, features // D_TILE, n))
    vmem = pl.BlockSpec(memory_space=pltpu.VMEM)
    hbm = pl.BlockSpec(memory_space=pl.ANY)
    weights = pltpu.VMEM((EXP_WIN, units, features), jnp.bfloat16)
    own, weighted = pl.pallas_call(
        functools.partial(kernel, n),
        out_shape=(
            jax.ShapeDtypeStruct((EXP_WIN * CAP, features), jnp.bfloat16),
            jax.ShapeDtypeStruct((EXP_WIN * CAP, tokens.shape[0]), jnp.bfloat16),
        ),
        in_specs=[vmem, vmem, vmem, hbm, hbm, hbm],
        out_specs=(vmem, vmem),
        scratch_shapes=[
            blocks,
            blocks,
            blocks,
            blocks,
            weights,
            weights,
            weights,
            pltpu.VMEM((n * ROWS, units), jnp.bfloat16),
            pltpu.VMEM((ROWS, D_TILE), jnp.float32),
            pltpu.SemaphoreType.DMA((3, EXP_WIN)),
            gather_semaphores,
            gather_semaphores,
            sum_semaphores,
            sum_semaphores,
        ],
        compiler_params=pltpu.CompilerParams(collective_id=0, has_side_effects=True, vmem_limit_bytes=60 * 2**20),
    )(tokens, expert_ids.T, route_logits.T, w_gate, w_up, w_down)
    mixed = lax.dot_general(weighted, own, (((0,), (0,)), ((), ())), preferred_element_type=jnp.float32)
    return mixed.astype(jnp.bfloat16)


def solution(mesh):
    in_specs = (
        P(("rep", "et"), None),
        P(("rep", "et"), None),
        P(("rep", "et"), None),
        P(None, "et", None),
        P(None, "et", None),
        P(None, "et", None),
    )
    out_specs = P(("rep", "et"), None)
    return jax.shard_map(
        functools.partial(body, mesh.shape["et"]), mesh=mesh, in_specs=in_specs, out_specs=out_specs, check_vma=False
    )
```

```python
import functools

import jax
import jax.numpy as jnp
from jax import lax
from jax.experimental import pallas as pl
from jax.experimental.pallas import tpu as pltpu
from jax.sharding import PartitionSpec as P

EXP_WIN = 2
CAP = 48
ROWS = 48
UNIT = 16
F_TILE = 256
D_TILE = 512
AG_INSIDE = 5
MESH = pl.DeviceIdType.MESH


def routing(ids, logits):
    rows, slots = ids.shape[1], EXP_WIN * CAP
    low, high = logits[0:1, :], logits[1:2, :]
    top = jnp.maximum(low, high)
    exp_low, exp_high = jnp.exp(low - top), jnp.exp(high - top)
    total = exp_low + exp_high
    prob_low = (exp_low / total).astype(jnp.bfloat16).astype(jnp.float32)
    prob_high = (exp_high / total).astype(jnp.bfloat16).astype(jnp.float32)
    slot = lax.broadcasted_iota(jnp.int32, (slots, rows), 0)
    expert = jnp.where(slot >= CAP, 1, 0)
    in_low, in_high = ids[0:1, :] == expert, ids[1:2, :] == expert
    weight = jnp.where(in_low, prob_low, 0.0) + jnp.where(in_high, prob_high, 0.0)
    routed = jnp.where(in_low, 1.0, 0.0) + jnp.where(in_high, 1.0, 0.0)
    upper = lax.broadcasted_iota(jnp.int32, (rows, rows), 0) <= lax.broadcasted_iota(jnp.int32, (rows, rows), 1)
    ranking = jnp.dot(
        routed.astype(jnp.bfloat16), jnp.where(upper, 1.0, 0.0).astype(jnp.bfloat16), preferred_element_type=jnp.float32
    )
    place = (slot - CAP * expert + 1).astype(jnp.float32)
    selected = jnp.where(ranking == place, routed, 0.0)
    return selected.astype(jnp.bfloat16), (selected * weight).astype(jnp.bfloat16)


def kernel(n, tokens, ids, logits, w_gate, w_up, w_down, own, weighted, *scratch):
    rows, terms, right, left, gate, up, down, hidden, total, load_sem, ag_send, ag_recv, rs_send, rs_recv = scratch
    p = lax.axis_index("et")
    features, units = tokens.shape[1], gate.shape[1]
    count, parts = EXP_WIN * CAP // ROWS, ROWS // UNIT
    per_expert = CAP // ROWS
    m = n * ROWS
    f_tile = F_TILE if units % F_TILE == 0 else units
    f_steps, d_steps = units // f_tile, features // D_TILE
    steps = f_steps + d_steps
    has_left, has_right = p > 0, p < n - 1

    def load(index, expert):
        source, held = ((w_gate, gate), (w_up, up), (w_down, down))[index]
        return pltpu.make_async_copy(source.at[expert], held.at[expert], load_sem.at[index, expert])

    for index in range(3):
        load(index, 0).start()

    barrier = pltpu.get_barrier_semaphore()

    @pl.when(has_left)
    def _():
        pl.semaphore_signal(barrier, inc=1, device_id={"et": p - 1}, device_id_type=MESH)

    @pl.when(has_right)
    def _():
        pl.semaphore_signal(barrier, inc=1, device_id={"et": p + 1}, device_id_type=MESH)

    plain, scaled = routing(ids[...], logits[...])
    weighted[...] = scaled
    for part in range(d_steps):
        columns = pl.ds(part * D_TILE, D_TILE)
        picked = jnp.dot(plain, tokens[:, columns], preferred_element_type=jnp.float32).astype(jnp.bfloat16)
        for c in range(count):
            rows[c, p, :, columns] = picked[c * ROWS : (c + 1) * ROWS]

    pl.semaphore_wait(barrier, jnp.where(has_left & has_right, 2, 1))

    def span(u):
        return pl.ds(pl.multiple_of(u * UNIT, UNIT), UNIT)

    def ag_copy(c, u, k, way, arriving=False):
        source = p - k if way == 0 else p + k
        held = rows.at[c, source, span(u)]
        step = k - 1 if arriving else k
        return pltpu.make_async_remote_copy(
            src_ref=held,
            dst_ref=held,
            send_sem=ag_send.at[way, c, u, step],
            recv_sem=ag_recv.at[way, c, u, step + 1],
            device_id={"et": p + 1 if (way == 0) != arriving else p - 1},
            device_id_type=MESH,
        )

    def ag_each(c, u, k, act):
        @pl.when((p - k >= 0) & has_right & (k < n - 1))
        def _():
            act(ag_copy(c, u, k, 0))

        @pl.when((p + k <= n - 1) & has_left & (k < n - 1))
        def _():
            act(ag_copy(c, u, k, 1))

    def ag_event(c, event):
        k, u = 1 + event // parts, event % parts

        @pl.when(p - k >= 0)
        def _():
            ag_copy(c, u, k, 0, True).wait_recv()

        @pl.when(p + k <= n - 1)
        def _():
            ag_copy(c, u, k, 1, True).wait_recv()

        ag_each(c, u, k, lambda copy: copy.start())

        @pl.when((k == max(n - 2, 1)) & (c + 1 < count))
        def _():
            ag_each(c + 1, u, 0, lambda copy: copy.start())

    def band(u):
        return pl.ds(pl.multiple_of(u * D_TILE, D_TILE), D_TILE)

    def rs_copy(c, u, k, way, arriving=False):
        held = (right, left)[way]
        step = k + 1 if arriving else k
        return pltpu.make_async_remote_copy(
            src_ref=held.at[c, step, :, band(u)],
            dst_ref=held.at[c, step - 1, :, band(u)],
            send_sem=rs_send.at[way, c, u, step],
            recv_sem=rs_recv.at[way, c, u, step - 1],
            device_id={"et": p + 1 if (way == 0) != arriving else p - 1},
            device_id_type=MESH,
        )

    def rs_event(c, event):
        k, u = n - 1 - event // d_steps, event % d_steps
        for way in range(2):
            held = (right, left)[way]
            target = p + k if way == 0 else p - k
            exists = target <= n - 1 if way == 0 else target >= 0
            behind = has_left if way == 0 else has_right

            @pl.when(exists & behind)
            def _():
                rs_copy(c, u, k, way, True).wait_recv()
                summed = held[c, k, :, band(u)].astype(jnp.float32) + terms[c, target, :, band(u)].astype(jnp.float32)
                held[c, k, :, band(u)] = summed.astype(jnp.bfloat16)

            @pl.when(exists & jnp.logical_not(behind))
            def _():
                held[c, k, :, band(u)] = terms[c, target, :, band(u)]

            @pl.when(exists)
            def _():
                rs_copy(c, u, k, way).start()

    ag_events = (n - 1) * parts
    ag_inside = min(ag_events, AG_INSIDE * ag_events // 9)
    rs_events = (n - 2) * d_steps

    @pl.loop(0, parts)
    def _(u):
        ag_each(0, u, 0, lambda copy: copy.start())

    for index in range(3):
        load(index, 1).start()

    @pl.loop(0, ag_events)
    def _(event):
        ag_event(0, event)

    @pl.loop(0, count)
    def _(c):
        expert = c // per_expert
        first_use = c % per_expert == 0

        @pl.loop(0, steps)
        def _(i):
            @pl.when((i == 0) & first_use)
            def _():
                load(0, expert).wait()
                load(1, expert).wait()

            @pl.when((i == f_steps) & first_use)
            def _():
                load(2, expert).wait()

            @pl.when(i < f_steps)
            def _():
                at = pl.ds(pl.multiple_of(i * f_tile, f_tile) if f_steps > 1 else 0, f_tile)
                x = rows[c].reshape(m, features)
                dims = (((1,), (1,)), ((), ()))
                g = lax.dot_general(x, gate[expert, at, :], dims, preferred_element_type=jnp.float32)
                u = lax.dot_general(x, up[expert, at, :], dims, preferred_element_type=jnp.float32)
                hidden[:, at] = (g / (1.0 + jnp.exp(-g)) * u).astype(jnp.bfloat16)

            @pl.when(i >= f_steps)
            def _():
                at = pl.ds(pl.multiple_of((i - f_steps) * D_TILE, D_TILE), D_TILE)
                y = jnp.dot(hidden[...], down[expert, :, at], preferred_element_type=jnp.float32)
                terms[c, :, :, at] = y.astype(jnp.bfloat16).reshape(n, ROWS, D_TILE)
                rs_event(c, i - f_steps)

            @pl.when(c > 0)
            def _():
                @pl.loop(i * rs_events // steps, (i + 1) * rs_events // steps)
                def _(event):
                    rs_event(c - 1, d_steps + event)

            @pl.when(c + 1 < count)
            def _():
                @pl.loop(i * ag_inside // steps, (i + 1) * ag_inside // steps)
                def _(event):
                    ag_event(c + 1, event)

        @pl.when(c + 1 < count)
        def _():
            @pl.loop(ag_inside, ag_events)
            def _(event):
                ag_event(c + 1, event)

    @pl.loop(d_steps, d_steps + rs_events)
    def _(event):
        rs_event(count - 1, event)

    @pl.loop(0, count * d_steps)
    def _(unit):
        c, u = unit // d_steps, unit % d_steps
        total[...] = terms[c, p, :, band(u)].astype(jnp.float32)

        @pl.when(has_left)
        def _():
            rs_copy(c, u, 0, 0, True).wait_recv()
            total[...] += right[c, 0, :, band(u)].astype(jnp.float32)

        @pl.when(has_right)
        def _():
            rs_copy(c, u, 0, 1, True).wait_recv()
            total[...] += left[c, 0, :, band(u)].astype(jnp.float32)

        own[pl.ds(pl.multiple_of(c * ROWS, ROWS), ROWS), band(u)] = total[...].astype(jnp.bfloat16)

    @pl.loop(0, n - 1)
    def _(k):
        @pl.loop(0, count * parts)
        def _(unit):
            ag_each(unit // parts, unit % parts, k, lambda copy: copy.wait_send())

        @pl.loop(0, count * d_steps)
        def _(unit):
            c, u = unit // d_steps, unit % d_steps

            @pl.when(p + k + 1 <= n - 1)
            def _():
                rs_copy(c, u, k + 1, 0).wait_send()

            @pl.when(p - k - 1 >= 0)
            def _():
                rs_copy(c, u, k + 1, 1).wait_send()


def body(n, tokens, expert_ids, route_logits, w_gate, w_up, w_down):
    count, features, units = EXP_WIN * CAP // ROWS, tokens.shape[1], w_gate.shape[1]
    blocks = pltpu.VMEM((count, n, ROWS, features), jnp.bfloat16)
    gather_semaphores = pltpu.SemaphoreType.DMA((2, count, ROWS // UNIT, n))
    sum_semaphores = pltpu.SemaphoreType.DMA((2, count, features // D_TILE, n))
    vmem = pl.BlockSpec(memory_space=pltpu.VMEM)
    hbm = pl.BlockSpec(memory_space=pl.ANY)
    weights = pltpu.VMEM((EXP_WIN, units, features), jnp.bfloat16)
    own, weighted = pl.pallas_call(
        functools.partial(kernel, n),
        out_shape=(
            jax.ShapeDtypeStruct((EXP_WIN * CAP, features), jnp.bfloat16),
            jax.ShapeDtypeStruct((EXP_WIN * CAP, tokens.shape[0]), jnp.bfloat16),
        ),
        in_specs=[vmem, vmem, vmem, hbm, hbm, hbm],
        out_specs=(vmem, vmem),
        scratch_shapes=[
            blocks,
            blocks,
            blocks,
            blocks,
            weights,
            weights,
            weights,
            pltpu.VMEM((n * ROWS, units), jnp.bfloat16),
            pltpu.VMEM((ROWS, D_TILE), jnp.float32),
            pltpu.SemaphoreType.DMA((3, EXP_WIN)),
            gather_semaphores,
            gather_semaphores,
            sum_semaphores,
            sum_semaphores,
        ],
        compiler_params=pltpu.CompilerParams(collective_id=0, has_side_effects=True, vmem_limit_bytes=60 * 2**20),
    )(tokens, expert_ids.T, route_logits.T, w_gate, w_up, w_down)
    mixed = lax.dot_general(weighted, own, (((0,), (0,)), ((), ())), preferred_element_type=jnp.float32)
    return mixed.astype(jnp.bfloat16)


def solution(mesh):
    in_specs = (
        P(("rep", "et"), None),
        P(("rep", "et"), None),
        P(("rep", "et"), None),
        P(None, "et", None),
        P(None, "et", None),
        P(None, "et", None),
    )
    out_specs = P(("rep", "et"), None)
    return jax.shard_map(
        functools.partial(body, mesh.shape["et"]), mesh=mesh, in_specs=in_specs, out_specs=out_specs, check_vma=False
    )
```
